32 devices in a mesh: seq: 8 (over y, x, core), head: 4 (over z).
Axes of the slice: x: 2, y: 2, z: 4, core: 2. Of those that a mesh axis runs over, the one named last changes fastest.
Arguments:
- spatial_qkv: bfloat16 [3, 16, 1024, 1152], P(None, 'seq', None, 'head'), may hold values from -300 to 300
- stream: bfloat16 [16, 1024, 1152], P('seq', None, 'head'), may hold values from -6 to 6
- out_spatial: bfloat16 [1152, 1152], P('head'), may hold values from -0.1875 to 0.1875
- qkv_temporal: bfloat16 [3, 1152, 1152], P(None, None, 'head'), may hold values from -16 to 16
- out_temporal: bfloat16 [1152, 1152], P('head'), may hold values from -0.1875 to 0.1875
- modulation: float32 [2, 4, 1152], replicated, may hold values from -2 to 2
- tok_count: int32 [2], replicated, may hold values from 128 to 1024, as said below
- frame_count: int32 [2], replicated, may hold values from 2 to 8, as said below
Outputs:
- result: bfloat16 [16, 1024, 1152], P(None, 'seq', 'head')
The draws below stay inside these ranges and needn't reach their ends.
Inputs may be any that keep to these rules, and one draw needn't show every extreme that they name: `tok_count`: the same count holds for every frame of a clip; some clip has exactly 1024. `frame_count`: some clip has exactly 8.
All inputs are finite; a program needn't handle non-finite values.
Results may differ from the reference program's by a relative error of at most 0.024.
Values may be sent and summed in bfloat16 or wider, within the bound.
No kernel may reach another device: no remote copies, remote signals or barrier semaphores. Data moves between devices by JAX's collectives and lax.ppermute only.
A program may use at most 128 MiB of HBM per device.

```python
import math
import jax
import jax.numpy as jnp
from jax import lax

HEADS = 16
HEAD_DIM = 72
D = 1152
FRAMES = 8
TOK = 1024
CF = 16
CLIPS = 2
N_HEAD = 4


def draw_spatial_qkv(key, part):
    key = jax.random.fold_in(key, 11)
    first, second, third = jax.random.split(key, 3)
    queries = jax.random.normal(first, (CF, TOK, D), jnp.float32)
    noise = jax.random.normal(second, (CF, TOK, D), jnp.float32)
    values = jax.random.normal(third, (CF, TOK, D), jnp.float32)
    key_rows = noise
    return jnp.stack([queries, key_rows, values]).astype(jnp.bfloat16)


def draw_qkv_temporal(key, part):
    key = jax.random.fold_in(key, 23)
    first, second, third = jax.random.split(key, 3)
    factor = 1.0 / math.sqrt(D)
    queries = factor * jax.random.normal(first, (D, D), jnp.float32)
    noise = factor * jax.random.normal(second, (D, D), jnp.float32)
    values = 2.0 * factor * jax.random.normal(third, (D, D), jnp.float32)
    key_rows = noise
    return jnp.stack([queries, key_rows, values]).astype(jnp.bfloat16)


def draw_tok_count(key, part):
    key = jax.random.fold_in(key, 37)
    first, second = jax.random.split(key)
    base = jax.random.randint(first, (CLIPS,), TOK // 8, TOK // 4 + 1)
    chosen = jax.random.randint(second, (), 0, CLIPS)
    return jnp.where(jnp.arange(CLIPS) == chosen, TOK, base).astype(jnp.int32)


def draw_frame_count(key, part):
    key = jax.random.fold_in(key, 41)
    first, second, third, fourth = jax.random.split(key, 4)
    base = jax.random.randint(first, (CLIPS,), FRAMES // 4, FRAMES + 1)
    chosen = jax.random.randint(second, (), 0, CLIPS)
    offset = jax.random.randint(third, (), 1, CLIPS)
    other = (chosen + offset) % CLIPS
    shorter = jax.random.randint(fourth, (), FRAMES // 4, FRAMES)
    clip_ids = jnp.arange(CLIPS)
    counts = jnp.where(clip_ids == other, shorter, base)
    return jnp.where(clip_ids == chosen, FRAMES, counts).astype(jnp.int32)


def level_of(rng, extent, cuts, smallest, largest):
    factor_of = 1.0
    for position, parts in cuts:
        steps = jax.random.uniform(jax.random.fold_in(jax.random.fold_in(rng, 6), position), (parts,), jnp.float32, smallest / len(cuts), largest / len(cuts))
        factor_of = factor_of * jnp.repeat(jnp.exp(steps), extent[position] // parts).reshape((-1,) + (1,) * (len(extent) - 1 - position))
    return factor_of


def scatter_about(key, dims, width, most, cuts=(), held_as=jnp.bfloat16):
    result = width * jax.random.normal(key, dims, jnp.float32)
    if cuts:
        result = result * level_of(key, dims, cuts, -0.22, 0.18)
    return jnp.clip(result, -most, most).astype(held_as)


def setup_inputs(seed: int = 0) -> dict:
    splits = jax.random.split(jax.random.key(seed), 9)
    return {
        "spatial_qkv": draw_spatial_qkv(jax.random.fold_in(splits[8], 71), 0),
        "stream": scatter_about(splits[1], (CF, TOK, D), 1.0, 6.0, ((0, 8), (2, 4))),
        "out_spatial": scatter_about(splits[2], (D, D), D ** -0.5, 0.1875, ((0, 4),)),
        "qkv_temporal": draw_qkv_temporal(jax.random.fold_in(splits[8], 71), 0),
        "out_temporal": scatter_about(splits[4], (D, D), D ** -0.5, 0.1875, ((0, 4),)),
        "modulation": scatter_about(splits[5], (CLIPS, 4, D), 0.5, 2.0, (), jnp.float32),
        "tok_count": draw_tok_count(jax.random.fold_in(splits[8], 71), 0),
        "frame_count": draw_frame_count(jax.random.fold_in(splits[8], 71), 0),
    }


def softmax_rows(scores):
    highest = lax.optimization_barrier(jnp.max(scores, axis=-1, keepdims=True))
    raised = jnp.exp(scores - highest)
    return raised / lax.optimization_barrier(jnp.sum(raised, axis=-1, keepdims=True))

def project_groups(rows, weight):
    group_width = rows.shape[1] // N_HEAD
    summed = jnp.zeros((rows.shape[0], weight.shape[1]), jnp.float32)
    for member in range(N_HEAD):
        lower = member * group_width
        partial_value = jnp.dot(rows[:, lower:lower + group_width], weight[lower:lower + group_width], preferred_element_type=jnp.float32).astype(jnp.bfloat16)
        partial_value = lax.optimization_barrier(partial_value)
        summed = summed + partial_value.astype(jnp.float32)
    return summed

def spatial_clip(inputs):
    queries, key_rows, values, count = inputs
    score_scale = 1.0 / math.sqrt(HEAD_DIM)
    scores = jnp.einsum('fqhd,fkhd->fhqk', queries.astype(jnp.float32), key_rows.astype(jnp.float32)) * score_scale
    live_keys = jnp.arange(TOK) < count
    scores = jnp.where(live_keys, scores, -jnp.inf)
    weights = softmax_rows(scores).astype(jnp.bfloat16)
    attended = jnp.einsum('fhqk,fkhd->fqhd', weights.astype(jnp.float32), values.astype(jnp.float32))
    return attended.astype(jnp.bfloat16)

def reference(spatial_qkv, stream, out_spatial, qkv_temporal, out_temporal, modulation, tok_count, frame_count):
    score_scale = 1.0 / math.sqrt(HEAD_DIM)
    stacked = spatial_qkv.reshape(3, CLIPS, FRAMES, TOK, HEADS, HEAD_DIM)
    attended = lax.map(spatial_clip, (stacked[0], stacked[1], stacked[2], tok_count))
    spatial_proj = project_groups(attended.reshape(CF * TOK, D), out_spatial).reshape(CLIPS, FRAMES, TOK, D)
    gate_spatial = modulation[:, 0][:, None, None, :]
    mixed_rows = (stream.reshape(CLIPS, FRAMES, TOK, D).astype(jnp.float32) + gate_spatial * spatial_proj).astype(jnp.bfloat16)
    full_rows = mixed_rows.astype(jnp.float32)
    center = full_rows - lax.optimization_barrier(jnp.mean(full_rows, axis=-1, keepdims=True))
    variance = lax.optimization_barrier(jnp.mean(center * center, axis=-1, keepdims=True))
    normed = center / jnp.sqrt(variance + 1e-06)
    normed = normed * (1.0 + modulation[:, 2][:, None, None, :]) + modulation[:, 1][:, None, None, :]
    normed = normed.astype(jnp.bfloat16).reshape(CF * TOK, D)
    projected = [jnp.dot(normed, qkv_temporal[member], preferred_element_type=jnp.float32).astype(jnp.bfloat16).reshape(CLIPS, FRAMES, TOK, HEADS, HEAD_DIM) for member in range(3)]
    scores = jnp.einsum('bfthd,bgthd->bthfg', projected[0].astype(jnp.float32), projected[1].astype(jnp.float32)) * score_scale
    live_frames = jnp.arange(FRAMES)[None, :] < frame_count[:, None]
    scores = jnp.where(live_frames[:, None, None, None, :], scores, -jnp.inf)
    weights = softmax_rows(scores).astype(jnp.bfloat16)
    temporal_attn = jnp.einsum('bthfg,bgthd->bfthd', weights.astype(jnp.float32), projected[2].astype(jnp.float32)).astype(jnp.bfloat16)
    temporal_proj = project_groups(temporal_attn.reshape(CF * TOK, D), out_temporal).reshape(CLIPS, FRAMES, TOK, D)
    output = mixed_rows.astype(jnp.float32) + modulation[:, 3][:, None, None, :] * temporal_proj
    live_tokens = jnp.arange(TOK)[None, :] < tok_count[:, None]
    valid = live_frames[:, :, None] & live_tokens[:, None, :]
    output = jnp.where(valid[..., None], output, 0.0)
    return output.astype(jnp.bfloat16).reshape(CF, TOK, D)
```

```python
import functools
import math

import jax
import jax.numpy as jnp
from jax import lax
from jax.experimental import pallas as pl
from jax.experimental.pallas import tpu as pltpu
from jax.sharding import Mesh
from jax.sharding import PartitionSpec as P

HEAD_DIM = 72
FRAMES = 8
PAIR = 2 * HEAD_DIM
KINDS = 3
SLICES = 8
EPS = 1e-6
F32 = jnp.float32
BF16 = jnp.bfloat16
VMEM_LIMIT = 48 * 1024 * 1024


def flip(array):
    return jnp.swapaxes(array, 0, 1)


def tn(lhs, rhs):
    return lax.dot_general(lhs, rhs, (((0,), (0,)), ((), ())), preferred_element_type=F32)


def runs_of(chunk, rank, sizes):
    groups, ranks, heads, block, span, run = sizes
    starts = []
    for piece in range(span // run):
        place = chunk * span + piece * run
        starts.append((place // block * ranks + rank) * block + place % block)
    return starts


def stream_kernel(sizes, info_ref, rows_ref, *out_refs):
    groups, ranks, heads, block, span, run = sizes
    me = info_ref[4]
    frames = rows_ref.shape[0]
    for chunk in range(heads):
        pieces = [
            rows_ref[frame, :, start:start + run]
            for rank in range(ranks) for frame in range(frames) for start in runs_of(chunk, rank, sizes)
        ]
        gathered = jnp.concatenate(pieces, axis=1)
        slot = lax.rem(chunk - me + heads, heads)
        for each in range(heads):
            @pl.when(slot == each)
            def store():
                out_refs[each][...] = gathered


def stream_chunks(info, stream, sizes):
    groups, ranks, heads, block, span, run = sizes
    frames, width, tokens = stream.shape
    rows = frames * tokens // heads
    vmem = pl.BlockSpec(memory_space=pltpu.VMEM)
    return pl.pallas_call(
        functools.partial(stream_kernel, sizes),
        in_specs=[pl.BlockSpec(memory_space=pltpu.SMEM), vmem],
        out_specs=[vmem] * heads,
        out_shape=[jax.ShapeDtypeStruct((width, rows), BF16)] * heads,
        compiler_params=pltpu.CompilerParams(vmem_limit_bytes=VMEM_LIMIT),
        name="stream_chunks",
    )(info, stream)


def arrange_kernel(sizes, info_ref, qkv_ref, query_ref, key_ref):
    groups, ranks, heads, block, span, run = sizes
    me = info_ref[4]
    for chunk in range(heads):
        pieces = [
            qkv_ref[0, 0, :, start:start + run]
            for rank in range(ranks) for start in runs_of(chunk, rank, sizes)
        ]
        slot = lax.rem(chunk - me + heads, heads)
        query_ref[slot, 0] = jnp.concatenate(pieces, axis=1)
    key_ref[0] = flip(qkv_ref[1, 0].astype(F32)).astype(BF16)


def arrange(info, qkv, sizes):
    groups, ranks, heads, block, span, run = sizes
    _, frames, width, tokens = qkv.shape
    return pl.pallas_call(
        functools.partial(arrange_kernel, sizes),
        grid_spec=pltpu.PrefetchScalarGridSpec(
            num_scalar_prefetch=1,
            grid=(frames,),
            in_specs=[pl.BlockSpec((2, 1, width, tokens), lambda f, info: (0, f, 0, 0))],
            out_specs=[
                pl.BlockSpec((heads, 1, width, tokens // heads), lambda f, info: (0, f, 0, 0)),
                pl.BlockSpec((1, tokens, width), lambda f, info: (f, 0, 0)),
            ],
        ),
        out_shape=[
            jax.ShapeDtypeStruct((heads, frames, width, tokens // heads), BF16),
            jax.ShapeDtypeStruct((frames, tokens, width), BF16),
        ],
        compiler_params=pltpu.CompilerParams(vmem_limit_bytes=VMEM_LIMIT),
        name="arrange",
    )(info, qkv)


def spatial_kernel(ranks, info_ref, query_ref, key_ref, value_ref, out_ref, part_ref):
    _, frames, width, per_frame = query_ref.shape
    tokens = key_ref.shape[1]
    local_heads = width // HEAD_DIM
    span = per_frame // ranks
    scale = math.log2(math.e) / math.sqrt(HEAD_DIM)
    count = info_ref[0]

    def attend(keys, masked):
        ones = jnp.ones((16, keys), BF16)
        for frame in range(frames):
            for head in range(local_heads):
                pair = head // 2
                low = (pair * PAIR) // 128 * 128
                high = min(-(-((pair + 1) * PAIR) // 128) * 128, width)
                row = lax.broadcasted_iota(jnp.int32, (high - low, per_frame), 0) + low
                mine = (row >= head * HEAD_DIM) & (row < (head + 1) * HEAD_DIM)
                query = jnp.where(mine, query_ref[0, frame, low:high, :], jnp.zeros((), BF16))
                scores = jnp.dot(key_ref[frame, :keys, low:high], query, preferred_element_type=F32)
                if masked:
                    token = lax.broadcasted_iota(jnp.int32, (keys, per_frame), 0)
                    scores = jnp.where(token < count, scores, -jnp.inf)
                highest = jnp.max(scores, axis=0, keepdims=True)
                raised = jnp.exp2(scores * scale - highest * scale).astype(BF16)
                values = jnp.concatenate(
                    [value_ref[0, frame, pair * PAIR:(pair + 1) * PAIR, :keys], ones], axis=0
                )
                summed = jnp.dot(values, raised, preferred_element_type=F32)
                inside = head % 2 * HEAD_DIM
                result = summed[inside:inside + HEAD_DIM] / summed[PAIR:PAIR + 1]
                for rank in range(ranks):
                    lane = (rank * frames + frame) * span
                    part_ref[head * HEAD_DIM:(head + 1) * HEAD_DIM, lane:lane + span] = (
                        result[:, rank * span:(rank + 1) * span]
                    )
        out_ref[...] = part_ref[...].astype(BF16)

    half = tokens // 2

    @pl.when(count >= tokens)
    def whole():
        attend(tokens, False)

    @pl.when((count < tokens) & (count > half))
    def some():
        attend(tokens, True)

    @pl.when(count <= half)
    def few():
        attend(half, True)


def spatial_attention(slot, info, queries, keys, qkv, ranks):
    heads, frames, width, per_frame = queries.shape
    rows = frames * per_frame
    return pl.pallas_call(
        functools.partial(spatial_kernel, ranks),
        grid_spec=pltpu.PrefetchScalarGridSpec(
            num_scalar_prefetch=1,
            grid=(1,),
            in_specs=[
                pl.BlockSpec((1, frames, width, per_frame), lambda c, info: (slot, 0, 0, 0)),
                pl.BlockSpec(keys.shape, lambda c, info: (0, 0, 0)),
                pl.BlockSpec((1,) + qkv.shape[1:], lambda c, info: (2, 0, 0, 0)),
            ],
            out_specs=pl.BlockSpec((width, rows), lambda c, info: (0, 0)),
            scratch_shapes=[pltpu.VMEM((width, rows), F32)],
        ),
        out_shape=jax.ShapeDtypeStruct((width, rows), BF16),
        compiler_params=pltpu.CompilerParams(vmem_limit_bytes=VMEM_LIMIT),
        name="spatial_attention",
    )(info, queries, keys, qkv)


def mix_kernel(heads, ranks, info_ref, near_ref, far_ref, gate_ref, *refs):
    att_refs, stream_refs, out_ref, sum_ref = refs[:heads], refs[heads:2 * heads], refs[-2], refs[-1]
    me = info_ref[4]
    core = info_ref[5]
    half = near_ref.shape[1]
    width = att_refs[0].shape[0]
    summed = None
    for step in range(heads):
        for which, weights in enumerate((near_ref, far_ref)):
            part = core if which == 0 else 1 - core
            rows = pl.ds(pl.multiple_of(part * half, half), half)
            term = tn(weights[step], att_refs[step][rows, :])
            summed = term if summed is None else summed + term
    sum_ref[...] = gate_ref[:, 0:1] * summed
    lanes = sum_ref.shape[1] // ranks
    for step in range(heads):
        source = lax.rem(me - step + heads, heads)
        rows = pl.ds(pl.multiple_of(source * width, width), width)
        mixed = (stream_refs[step][...].astype(F32) + sum_ref[rows, :]).astype(BF16)
        for rank in range(ranks):
            out_ref[rank, rows, :] = mixed[:, rank * lanes:(rank + 1) * lanes]


def mix(info, near, far, attended, stream, columns, ranks):
    heads = len(attended)
    width, rows = attended[0].shape
    features = near.shape[2]
    vmem = pl.BlockSpec(memory_space=pltpu.VMEM)
    return pl.pallas_call(
        functools.partial(mix_kernel, heads, ranks),
        in_specs=[pl.BlockSpec(memory_space=pltpu.SMEM)] + [vmem] * (3 + 2 * heads),
        out_specs=vmem,
        out_shape=jax.ShapeDtypeStruct((ranks, features, rows // ranks), BF16),
        scratch_shapes=[pltpu.VMEM((features, rows), F32)],
        compiler_params=pltpu.CompilerParams(vmem_limit_bytes=VMEM_LIMIT),
        name="mix",
    )(info, near, far, columns, *attended, *stream)


def temporal_kernel(sizes, info_ref, mixed_ref, cols_ref, q_ref, k_ref, v_ref, o_ref, *refs):
    groups, ranks, heads, block, span, run = sizes
    out_refs, normed_ref, total_ref, result_ref = refs[:-3], refs[-3], refs[-2], refs[-1]
    step = pl.program_id(0)
    _, features, lanes = mixed_ref.shape
    rows = ranks * lanes
    scale = 1.0 / math.sqrt(HEAD_DIM)
    frame_count = info_ref[1]

    @pl.when(step == 0)
    def norm():
        for rank in range(ranks):
            full = mixed_ref[rank].astype(F32)
            center = full - jnp.mean(full, axis=0, keepdims=True)
            variance = jnp.mean(center * center, axis=0, keepdims=True)
            normed = center * lax.rsqrt(variance + EPS)
            normed = normed * (1.0 + cols_ref[:, 2:3]) + cols_ref[:, 1:2]
            normed_ref[:, rank * lanes:(rank + 1) * lanes] = normed.astype(BF16)

    weights = jnp.concatenate([q_ref[0, 0], k_ref[0, 0], v_ref[0, 0]], axis=0)
    projected = jnp.dot(weights, normed_ref[...], preferred_element_type=F32)
    frame = lax.broadcasted_iota(jnp.int32, (FRAMES, rows), 1) // span
    delta = lax.broadcasted_iota(jnp.int32, (FRAMES, rows), 0)
    key_frame = lax.rem(frame - delta + FRAMES, FRAMES)
    live = key_frame < frame_count

    def turned(array):
        return [array if d == 0 else pltpu.roll(array, d * span, 1) for d in range(FRAMES)]

    attended = []
    for head in range(2):
        query = projected[head * HEAD_DIM:(head + 1) * HEAD_DIM]
        key = projected[PAIR + head * HEAD_DIM:PAIR + (head + 1) * HEAD_DIM]
        value = projected[2 * PAIR + head * HEAD_DIM:2 * PAIR + (head + 1) * HEAD_DIM]
        scores = [jnp.sum(query * each, axis=0, keepdims=True) for each in turned(key)]
        scores = jnp.concatenate(scores, axis=0) * scale
        scores = jnp.where(live, scores, -jnp.inf)
        raised = jnp.exp(scores - jnp.max(scores, axis=0, keepdims=True))
        shares = raised / jnp.sum(raised, axis=0, keepdims=True)
        summed = None
        for d, each in enumerate(turned(value)):
            term = shares[d:d + 1] * each
            summed = term if summed is None else summed + term
        attended.append(summed)
    attended = jnp.concatenate(attended, axis=0).astype(BF16)
    term = tn(o_ref[0, 0], attended)

    @pl.when(step == 0)
    def first():
        total_ref[...] = term

    @pl.when(step > 0)
    def later():
        total_ref[...] += term

    @pl.when(step == pl.num_programs(0) - 1)
    def finish():
        width = features // heads
        clip, rank_here, me, count = info_ref[2], info_ref[3], info_ref[4], info_ref[0]
        for rank in range(ranks):
            lane = slice(rank * lanes, (rank + 1) * lanes)
            full = mixed_ref[rank].astype(F32) + cols_ref[:, 3:4] * total_ref[:, lane]
            place = lax.broadcasted_iota(jnp.int32, (1, lanes), 1) + rank * lanes
            among = me * span + place % span
            token = (among // block * ranks + rank_here) * block + among % block
            valid = (place // span < frame_count) & (token < count)
            result_ref[:, lane] = jnp.where(valid, full, 0.0).astype(BF16)
        parts = span // run
        share = max(heads // groups, 1)
        for part in range(parts):
            slot = lax.rem(part + parts - lax.rem(clip, parts), parts)
            turn = clip * share if parts == 1 else clip // parts
            for step_to in range(heads):
                to = lax.rem(me * (parts == 1) + step_to + turn, heads)
                rows_to = pl.ds(pl.multiple_of(to * width, width), width)

                def pick():
                    if parts == 1:
                        return result_ref[rows_to, :]
                    found = result_ref[rows_to, :]
                    return jnp.concatenate(
                        [found[:, f * span + part * run:f * span + (part + 1) * run] for f in range(FRAMES)], axis=1
                    )

                for each in range(parts):
                    @pl.when(slot == each)
                    def store():
                        out_refs[each * heads + step_to][...] = pick()


def temporal(info, mixed, columns, pieces, sizes):
    groups, ranks, heads, block, span, run = sizes
    _, features, lanes = mixed.shape
    rows = ranks * lanes
    pairs = SLICES // (KINDS + 1)
    count = heads * (span // run)
    shape = (features // heads, FRAMES * run)

    def piece(kind):
        return pl.BlockSpec(
            (1, 1, PAIR, features), lambda s, info: (kind * pairs + s % pairs, s // pairs, 0, 0)
        )

    return pl.pallas_call(
        functools.partial(temporal_kernel, sizes),
        grid_spec=pltpu.PrefetchScalarGridSpec(
            num_scalar_prefetch=1,
            grid=(heads * pairs,),
            in_specs=[
                pl.BlockSpec(mixed.shape, lambda s, info: (0, 0, 0)),
                pl.BlockSpec(columns.shape, lambda s, info: (0, 0)),
                piece(0),
                piece(1),
                piece(2),
                piece(3),
            ],
            out_specs=[pl.BlockSpec(shape, lambda s, info: (0, 0))] * count,
            scratch_shapes=[
                pltpu.VMEM((features, rows), BF16),
                pltpu.VMEM((features, rows), F32),
                pltpu.VMEM((features, rows), BF16),
            ],
        ),
        out_shape=[jax.ShapeDtypeStruct(shape, BF16)] * count,
        compiler_params=pltpu.CompilerParams(vmem_limit_bytes=VMEM_LIMIT),
        name="temporal",
    )(info, mixed, columns, pieces, pieces, pieces, pieces)


def place_kernel(sizes, info_ref, *refs):
    groups, ranks, heads, block, span, run = sizes
    parts = span // run
    share = block // run
    piece_refs, out_ref, held_ref = refs[:-2], refs[-2], refs[-1]
    clip, me = info_ref[2], info_ref[4]
    for part in range(parts):
        for step in range(heads):
            if parts == 1:
                source = lax.rem(me - step + heads + groups * heads - clip * share, heads)
            else:
                source = lax.rem(me - step + heads, heads) * parts + lax.rem(clip - part + parts, parts)
            held_ref[source] = piece_refs[part * heads + step][...]
    for group in range(groups):
        for frame in range(FRAMES):
            pieces = [held_ref[group * share + e, :, frame * run:(frame + 1) * run] for e in range(share)]
            out_ref[group * FRAMES + frame] = jnp.concatenate(pieces, axis=1) if share > 1 else pieces[0]


def place(info, pieces, sizes):
    groups, ranks, heads, block, span, run = sizes
    width, lanes = pieces[0].shape
    vmem = pl.BlockSpec(memory_space=pltpu.VMEM)
    return pl.pallas_call(
        functools.partial(place_kernel, sizes),
        in_specs=[pl.BlockSpec(memory_space=pltpu.SMEM)] + [vmem] * len(pieces),
        out_specs=vmem,
        out_shape=jax.ShapeDtypeStruct((groups * FRAMES, width, block), BF16),
        scratch_shapes=[pltpu.VMEM((len(pieces), width, lanes), BF16)],
        compiler_params=pltpu.CompilerParams(vmem_limit_bytes=VMEM_LIMIT),
        name="place",
    )(info, *pieces)


def routes(step, part, sizes):
    groups, ranks, heads, block, span, run = sizes
    parts = span // run
    share = block // run
    pairs = []
    for clip in range(groups):
        for head in range(heads):
            if parts == 1:
                to = (head // share, (head + step + clip * share) % heads)
            else:
                to = (head * parts + (part + clip) % parts, (step + clip // parts) % heads)
            pairs.append((clip * heads + head, to[0] * heads + to[1]))
    return pairs


def on_device(
    shape, spatial_qkv, stream, out_spatial, qkv_temporal, out_temporal, modulation, tok_count, frame_count
):
    outer, clips_inner, rank_hi, cores, heads = shape
    groups = outer * clips_inner
    ranks = rank_hi * cores
    clip = lax.axis_index(("outer", "clip"))
    rank = lax.axis_index(("rank", "core"))
    core = lax.axis_index("core")
    head = lax.axis_index("head")
    member = lax.axis_index(("clip", "rank", "core"))
    width = spatial_qkv.shape[3]
    features = out_spatial.shape[1]
    frames, tokens = stream.shape[:2]
    block = tokens // (groups * ranks)
    span = tokens // (ranks * heads)
    run = min(block, span)
    sizes = (groups, ranks, heads, block, span, run)
    rings = [[(i, (i + k) % heads) for i in range(heads)] for k in range(heads)]

    def to_heads(arrays):
        return [arrays[0]] + [lax.ppermute(arrays[k], "head", rings[k]) for k in range(1, heads)]

    info = jnp.stack([tok_count[clip], frame_count[clip], clip, rank, head, core]).astype(jnp.int32)
    stream_sent = stream_chunks(info, jnp.swapaxes(stream, 1, 2), sizes)

    half = width // cores
    near = lax.dynamic_slice(out_spatial, (core * half, 0), (half, features))
    near = jnp.stack(to_heads([near] * heads))
    far = lax.ppermute(near, "core", [(0, 1), (1, 0)])

    pairs = SLICES // (KINDS + 1)
    kind = jnp.minimum(member // pairs, KINDS - 1)
    pair = member % pairs
    turned = jnp.swapaxes(qkv_temporal, 1, 2)
    weight = lax.dynamic_slice(turned, (kind, pair * PAIR, 0), (1, PAIR, features))[0]
    other = lax.dynamic_slice(out_temporal, (pair * PAIR, 0), (PAIR, features))
    mine = jnp.where(member < KINDS * pairs, weight, other)
    pieces = lax.all_gather(mine, ("clip", "rank", "core", "head"))
    pieces = pieces.reshape(SLICES, heads, PAIR, features)

    here = lax.dynamic_index_in_dim(modulation, clip, 0, keepdims=False)
    columns = here.T

    stream_sent, info = lax.optimization_barrier((stream_sent, info))
    stream_rows = to_heads(stream_sent)

    qkv = jnp.swapaxes(spatial_qkv, 2, 3)
    queries, keys = arrange(info, qkv, sizes)
    attended = [None] * heads
    for k in list(range(1, heads)) + [0]:
        attended[k] = spatial_attention(k, info, queries, keys, qkv, ranks)
        attended[k], info = lax.optimization_barrier((attended[k], info))
    attended = to_heads(attended)
    mixed = mix(info, near, far, attended, stream_rows, columns, ranks)
    mixed = lax.all_to_all(mixed, ("rank", "core"), 0, 0)
    result = temporal(info, mixed, columns, pieces, sizes)
    arrived = [
        lax.ppermute(result[part * heads + step], ("outer", "clip", "head"), routes(step, part, sizes))
        for part in range(span // run) for step in range(heads)
    ]
    return jnp.swapaxes(place(info, arrived, sizes), 1, 2)


def solution(mesh):
    seq, heads = mesh.shape["seq"], mesh.shape["head"]

    def whole(spatial_qkv, stream, *rest):
        frames = spatial_qkv.shape[1] // seq
        ranks = FRAMES // frames
        clips_inner = SLICES // ranks
        shape = (seq // SLICES, clips_inner, ranks // 2, 2, heads)
        fine = Mesh(mesh.devices.reshape(shape), ("outer", "clip", "rank", "core", "head"))
        split = ("outer", "clip", "rank", "core")
        in_specs = (
            P(None, split, None, "head"),
            P(split, None, "head"),
            P("head", None),
            P(None, None, "head"),
            P("head", None),
            P(),
            P(),
            P(),
        )
        return jax.shard_map(
            functools.partial(on_device, shape), mesh=fine, in_specs=in_specs, out_specs=P(None, split, "head"),
            check_vma=False,
        )(spatial_qkv, stream, *rest)

    return whole
```

```python
import functools
import math

import jax
import jax.numpy as jnp
from jax import lax
from jax.experimental import pallas as pl
from jax.experimental.pallas import tpu as pltpu
from jax.sharding import Mesh
from jax.sharding import PartitionSpec as P

HEAD_DIM = 72
FRAMES = 8
PAIR = 2 * HEAD_DIM
KINDS = 3
SLICES = 8
EPS = 1e-6
F32 = jnp.float32
BF16 = jnp.bfloat16
MIB = 1024 * 1024


def flip(array):
    return jnp.swapaxes(array, 0, 1)


def tn(lhs, rhs):
    return lax.dot_general(lhs, rhs, (((0,), (0,)), ((), ())), preferred_element_type=F32)


def runs_of(chunk, rank, sizes):
    groups, ranks, heads, block, span, run = sizes
    starts = []
    for piece in range(span // run):
        place = chunk * span + piece * run
        starts.append((place // block * ranks + rank) * block + place % block)
    return starts


def spatial_kernel(sizes, info_ref, qkv_ref, stream_ref, out_ref, query_ref, key_ref, value_ref, part_ref):
    groups, ranks, heads, block, span, run = sizes
    chunk = pl.program_id(0)
    _, frames, width, tokens = qkv_ref.shape
    pairs = width // PAIR
    per_frame = tokens // heads
    scale = math.log2(math.e) / math.sqrt(HEAD_DIM)
    count = info_ref[0]

    @pl.when(chunk == 0)
    def arrange():
        for each in range(heads):
            for frame in range(frames):
                pieces = [
                    qkv_ref[0, frame, :, start:start + run]
                    for rank in range(ranks) for start in runs_of(each, rank, sizes)
                ]
                query_ref[each, frame] = jnp.concatenate(pieces, axis=1)
            pieces = [
                stream_ref[frame, :, start:start + run]
                for rank in range(ranks) for frame in range(frames) for start in runs_of(each, rank, sizes)
            ]
            out_ref[each, width:, :] = jnp.concatenate(pieces, axis=1)
        for frame in range(frames):
            key_ref[frame] = flip(qkv_ref[1, frame].astype(F32)).astype(BF16)
            for pair in range(pairs):
                value_ref[frame, pair, :PAIR, :] = qkv_ref[2, frame, pair * PAIR:(pair + 1) * PAIR, :]
                value_ref[frame, pair, PAIR:, :] = jnp.ones((value_ref.shape[2] - PAIR, tokens), BF16)

    def attend(keys, masked):
        for frame in range(frames):
            for head in range(2 * pairs):
                pair = head // 2
                low = (pair * PAIR) // 128 * 128
                high = min(-(-((pair + 1) * PAIR) // 128) * 128, width)
                row = lax.broadcasted_iota(jnp.int32, (high - low, per_frame), 0) + low
                mine = (row >= head * HEAD_DIM) & (row < (head + 1) * HEAD_DIM)
                query = jnp.where(mine, query_ref[chunk, frame, low:high, :], jnp.zeros((), BF16))
                scores = jnp.dot(key_ref[frame, :keys, low:high], query, preferred_element_type=F32)
                if masked:
                    token = lax.broadcasted_iota(jnp.int32, (keys, per_frame), 0)
                    scores = jnp.where(token < count, scores, -jnp.inf)
                highest = jnp.max(scores, axis=0, keepdims=True)
                raised = jnp.exp2(scores * scale - highest * scale).astype(BF16)
                summed = jnp.dot(value_ref[frame, pair, :, :keys], raised, preferred_element_type=F32)
                inside = head % 2 * HEAD_DIM
                result = summed[inside:inside + HEAD_DIM] / summed[PAIR:PAIR + 1]
                for rank in range(ranks):
                    lane = (rank * frames + frame) * span
                    part_ref[head * HEAD_DIM:(head + 1) * HEAD_DIM, lane:lane + span] = (
                        result[:, rank * span:(rank + 1) * span]
                    )

    half = tokens // 2

    @pl.when(count >= tokens)
    def whole():
        attend(tokens, False)

    @pl.when((count < tokens) & (count > half))
    def some():
        attend(tokens, True)

    @pl.when(count <= half)
    def few():
        attend(half, True)

    out_ref[chunk, :width, :] = part_ref[...].astype(BF16)


def spatial_attention(info, qkv, stream, sizes):
    groups, ranks, heads, block, span, run = sizes
    _, frames, width, tokens = qkv.shape
    rows = frames * tokens // heads
    pairs = width // PAIR
    vmem = pl.BlockSpec(memory_space=pltpu.VMEM)
    return pl.pallas_call(
        functools.partial(spatial_kernel, sizes),
        grid_spec=pltpu.PrefetchScalarGridSpec(
            num_scalar_prefetch=1,
            grid=(heads,),
            in_specs=[vmem, vmem],
            out_specs=vmem,
            scratch_shapes=[
                pltpu.VMEM((heads, frames, width, tokens // heads), BF16),
                pltpu.VMEM((frames, tokens, width), BF16),
                pltpu.VMEM((frames, pairs, PAIR + 16, tokens), BF16),
                pltpu.VMEM((width, rows), F32),
            ],
        ),
        out_shape=jax.ShapeDtypeStruct((heads, 2 * width, rows), BF16),
        compiler_params=pltpu.CompilerParams(vmem_limit_bytes=24 * MIB),
        cost_estimate=pl.CostEstimate(flops=28 * 10**9, bytes_accessed=5 * 10**6, transcendentals=8 * 10**6),
        name="spatial_attention",
    )(info, qkv, stream)


def mix_kernel(heads, ranks, info_ref, plane_ref, core_ref, gate_ref, rows_ref, *refs):
    out_refs, weight_ref, mixed_ref = refs[:-2], refs[-2], refs[-1]
    rank, me, core, member = info_ref[3], info_ref[4], info_ref[5], info_ref[6]
    members, _, strip, _ = plane_ref.shape
    width = rows_ref.shape[1] // 2
    half = weight_ref.shape[0] // (2 * heads)
    last = half // strip - 1
    for far, ref in enumerate((plane_ref, core_ref)):
        for other in range(members):
            whose = jnp.minimum(member ^ other, last)
            for step in range(heads):
                source = lax.rem(me - step + heads, heads)
                start = source * width + (core ^ far) * half + whose * strip
                weight_ref[pl.ds(pl.multiple_of(start, 16), strip), :] = ref[other, step]
    summed = None
    for source in range(heads):
        term = tn(weight_ref[source * width:(source + 1) * width, :], rows_ref[source, :width, :])
        summed = term if summed is None else summed + term
    for source in range(heads):
        here = slice(source * width, (source + 1) * width)
        mixed = rows_ref[source, width:, :].astype(F32) + gate_ref[here, 0:1] * summed[here]
        mixed_ref[here, :] = mixed.astype(BF16)
    lanes = mixed_ref.shape[1] // ranks
    for step in range(ranks):
        to = lax.rem(rank + step, ranks)
        out_refs[step][...] = mixed_ref[:, pl.ds(pl.multiple_of(to * lanes, lanes), lanes)]


def mix(info, by_plane, by_core, arrived, columns, ranks):
    heads, width, rows = arrived.shape
    width = width // 2
    features = by_plane.shape[3]
    vmem = pl.BlockSpec(memory_space=pltpu.VMEM)
    return pl.pallas_call(
        functools.partial(mix_kernel, heads, ranks),
        in_specs=[pl.BlockSpec(memory_space=pltpu.SMEM)] + [vmem] * 4,
        out_specs=[vmem] * ranks,
        out_shape=[jax.ShapeDtypeStruct((features, rows // ranks), BF16)] * ranks,
        scratch_shapes=[pltpu.VMEM((heads * width, features), BF16), pltpu.VMEM((features, rows), BF16)],
        compiler_params=pltpu.CompilerParams(vmem_limit_bytes=28 * MIB),
        cost_estimate=pl.CostEstimate(flops=5 * 10**9, bytes_accessed=4 * 10**6, transcendentals=0),
        name="mix",
    )(info, by_plane, by_core, columns, arrived)


def frame_at(place, rank, sizes):
    ranks = sizes[1]
    frames = FRAMES // ranks
    return lax.rem(rank - place // frames + ranks, ranks) * frames + place % frames


def temporal_kernel(sizes, info_ref, cols_ref, *refs):
    groups, ranks, heads, block, span, run = sizes
    kinds = KINDS + 1
    mixed_refs, refs = refs[:ranks], refs[ranks:]
    piece_refs, out_refs = refs[:kinds], refs[kinds:-5]
    normed_ref, attended_ref, result_ref, weight_ref, last_ref = refs[-5:]
    step = pl.program_id(0)
    features, lanes = mixed_refs[0].shape
    rows = ranks * lanes
    scale = 1.0 / math.sqrt(HEAD_DIM)
    frame_count = info_ref[1]
    rank_here = info_ref[3]

    @pl.when(step == 0)
    def norm():
        for rank in range(ranks):
            full = mixed_refs[rank][...].astype(F32)
            center = full - jnp.mean(full, axis=0, keepdims=True)
            variance = jnp.mean(center * center, axis=0, keepdims=True)
            normed = center * lax.rsqrt(variance + EPS)
            normed = normed * (1.0 + cols_ref[:, 2:3]) + cols_ref[:, 1:2]
            normed_ref[:, rank * lanes:(rank + 1) * lanes] = normed.astype(BF16)

    for kind in range(KINDS):
        weight_ref[kind * PAIR:(kind + 1) * PAIR, :] = piece_refs[kind][0, 0]
    here = pl.ds(pl.multiple_of(step * PAIR, PAIR), PAIR)
    last_ref[here, :] = piece_refs[KINDS][0, 0]
    projected = jnp.dot(weight_ref[...], normed_ref[...], preferred_element_type=F32)
    frame = lax.broadcasted_iota(jnp.int32, (FRAMES, rows), 1) // span
    delta = lax.broadcasted_iota(jnp.int32, (FRAMES, rows), 0)
    key_frame = frame_at(lax.rem(frame - delta + FRAMES, FRAMES), rank_here, sizes)
    live = key_frame < frame_count

    def turned(array):
        return [array if d == 0 else pltpu.roll(array, d * span, 1) for d in range(FRAMES)]

    attended = []
    for head in range(2):
        query = projected[head * HEAD_DIM:(head + 1) * HEAD_DIM]
        key = projected[PAIR + head * HEAD_DIM:PAIR + (head + 1) * HEAD_DIM]
        value = projected[2 * PAIR + head * HEAD_DIM:2 * PAIR + (head + 1) * HEAD_DIM]
        scores = [jnp.sum(query * each, axis=0, keepdims=True) for each in turned(key)]
        scores = jnp.concatenate(scores, axis=0) * scale
        scores = jnp.where(live, scores, -jnp.inf)
        raised = jnp.exp(scores - jnp.max(scores, axis=0, keepdims=True))
        shares = raised / jnp.sum(raised, axis=0, keepdims=True)
        summed = None
        for d, each in enumerate(turned(value)):
            term = shares[d:d + 1] * each
            summed = term if summed is None else summed + term
        attended.append(summed)
    attended_ref[here, :] = jnp.concatenate(attended, axis=0).astype(BF16)

    @pl.when(step == pl.num_programs(0) - 1)
    def finish():
        width = features // heads
        clip, me, count = info_ref[2], info_ref[4], info_ref[0]
        total = tn(last_ref[...], attended_ref[...])
        for rank in range(ranks):
            lane = slice(rank * lanes, (rank + 1) * lanes)
            full = mixed_refs[rank][...].astype(F32) + cols_ref[:, 3:4] * total[:, lane]
            place = lax.broadcasted_iota(jnp.int32, (1, lanes), 1) + rank * lanes
            among = me * span + place % span
            token = (among // block * ranks + rank_here) * block + among % block
            valid = (frame_at(place // span, rank_here, sizes) < frame_count) & (token < count)
            result_ref[:, lane] = jnp.where(valid, full, 0.0).astype(BF16)
        parts = span // run
        share = max(heads // groups, 1)
        for part in range(parts):
            slot = lax.rem(part + parts - lax.rem(clip, parts), parts)
            turn = clip * share if parts == 1 else clip // parts
            for step_to in range(heads):
                to = lax.rem(me * (parts == 1) + step_to + turn, heads)
                rows_to = pl.ds(pl.multiple_of(to * width, width), width)

                def pick():
                    if parts == 1:
                        return result_ref[rows_to, :]
                    found = result_ref[rows_to, :]
                    return jnp.concatenate(
                        [found[:, f * span + part * run:f * span + (part + 1) * run] for f in range(FRAMES)], axis=1
                    )

                for each in range(parts):
                    @pl.when(slot == each)
                    def store():
                        out_refs[each * heads + step_to][...] = pick()


def temporal(info, mixed, columns, pieces, sizes):
    groups, ranks, heads, block, span, run = sizes
    features, lanes = mixed[0].shape
    rows = ranks * lanes
    kinds = KINDS + 1
    count = heads * (span // run)
    shape = (features // heads, FRAMES * run)

    def piece(kind):
        return pl.BlockSpec((1, 1, PAIR, features), lambda s, info: (2 * kind + s % 2, s // 2, 0, 0))

    return pl.pallas_call(
        functools.partial(temporal_kernel, sizes),
        grid_spec=pltpu.PrefetchScalarGridSpec(
            num_scalar_prefetch=1,
            grid=(2 * heads,),
            in_specs=[
                pl.BlockSpec(columns.shape, lambda s, info: (0, 0)),
            ] + [pl.BlockSpec(memory_space=pltpu.VMEM)] * ranks + [piece(kind) for kind in range(kinds)],
            out_specs=[pl.BlockSpec(shape, lambda s, info: (0, 0))] * count,
            scratch_shapes=[
                pltpu.VMEM((features, rows), BF16),
                pltpu.VMEM((features, rows), BF16),
                pltpu.VMEM((features, rows), BF16),
                pltpu.VMEM((KINDS * PAIR, features), BF16),
                pltpu.VMEM((features, features), BF16),
            ],
        ),
        out_shape=[jax.ShapeDtypeStruct(shape, BF16)] * count,
        compiler_params=pltpu.CompilerParams(vmem_limit_bytes=56 * MIB),
        cost_estimate=pl.CostEstimate(flops=20 * 10**9, bytes_accessed=12 * 10**6, transcendentals=0),
        name="temporal",
    )(info, columns, *mixed, *[pieces] * kinds)


def place_kernel(sizes, info_ref, *refs):
    groups, ranks, heads, block, span, run = sizes
    parts = span // run
    share = block // run
    piece_refs, out_ref, held_ref = refs[:-2], refs[-2], refs[-1]
    clip, rank, me = info_ref[2], info_ref[3], info_ref[4]
    for part in range(parts):
        for step in range(heads):
            if parts == 1:
                source = lax.rem(me - step + heads + groups * heads - clip * share, heads)
            else:
                source = lax.rem(me - step + heads, heads) * parts + lax.rem(clip - part + parts, parts)
            held_ref[source] = piece_refs[part * heads + step][...]
    for group in range(groups):
        for at in range(FRAMES):
            pieces = [held_ref[group * share + e, :, at * run:(at + 1) * run] for e in range(share)]
            out_ref[group * FRAMES + frame_at(at, rank, sizes)] = jnp.concatenate(pieces, axis=1) if share > 1 else pieces[0]


def place(info, pieces, sizes):
    groups, ranks, heads, block, span, run = sizes
    width, lanes = pieces[0].shape
    vmem = pl.BlockSpec(memory_space=pltpu.VMEM)
    return pl.pallas_call(
        functools.partial(place_kernel, sizes),
        in_specs=[pl.BlockSpec(memory_space=pltpu.SMEM)] + [vmem] * len(pieces),
        out_specs=vmem,
        out_shape=jax.ShapeDtypeStruct((groups * FRAMES, width, block), BF16),
        scratch_shapes=[pltpu.VMEM((len(pieces), width, lanes), BF16)],
        compiler_params=pltpu.CompilerParams(vmem_limit_bytes=12 * MIB),
        name="place",
    )(info, *pieces)


def routes(step, part, sizes):
    groups, ranks, heads, block, span, run = sizes
    parts = span // run
    share = block // run
    pairs = []
    for clip in range(groups):
        for head in range(heads):
            if parts == 1:
                to = (head // share, (head + step + clip * share) % heads)
            else:
                to = (head * parts + (part + clip) % parts, (step + clip // parts) % heads)
            pairs.append((clip * heads + head, to[0] * heads + to[1]))
    return pairs


def on_device(
    shape, spatial_qkv, stream, out_spatial, qkv_temporal, out_temporal, modulation, tok_count, frame_count
):
    outer, clips_inner, rank_hi, cores, heads = shape
    groups = outer * clips_inner
    ranks = rank_hi * cores
    assert cores == 2 and clips_inner * rank_hi == KINDS + 1
    clip = lax.axis_index(("outer", "clip"))
    rank = lax.axis_index(("rank", "core"))
    core = lax.axis_index("core")
    head = lax.axis_index("head")
    member = lax.axis_index(("clip", "rank"))
    width = spatial_qkv.shape[3]
    features = out_spatial.shape[1]
    frames, tokens = stream.shape[:2]
    block = tokens // (groups * ranks)
    span = tokens // (ranks * heads)
    run = min(block, span)
    sizes = (groups, ranks, heads, block, span, run)

    def send(array, axis, size, step):
        return lax.ppermute(array, axis, [(i, (i + step) % size) for i in range(size)])

    def around(arrays, axis, size):
        return [arrays[0]] + [send(arrays[k], axis, size, k) for k in range(1, size)]

    def swap(array, axis, size, bit):
        return lax.ppermute(array, axis, [(i, i ^ bit) for i in range(size)])

    info = jnp.stack([tok_count[clip], frame_count[clip], clip, rank, head, core, member]).astype(jnp.int32)
    here = lax.dynamic_index_in_dim(modulation, clip, 0, keepdims=False)
    columns = here.T

    plane = clips_inner * rank_hi
    turned = jnp.swapaxes(qkv_temporal, 1, 2)
    weight = lax.dynamic_slice(turned, (jnp.minimum(member, KINDS - 1), core * PAIR, 0), (1, PAIR, features))[0]
    other = lax.dynamic_slice(out_temporal, (core * PAIR, 0), (PAIR, features))
    weight = jnp.where(member < KINDS, weight, other)
    half = width // cores
    strip = half // KINDS
    spatial = lax.dynamic_slice(
        out_spatial, (core * half + jnp.minimum(member, KINDS - 1) * strip, 0), (strip, features)
    )
    mine = jnp.concatenate([weight, spatial], axis=0)
    mine, info = lax.optimization_barrier((mine, info))
    mine = around([mine] * heads, "head", heads)
    attended = spatial_attention(info, jnp.swapaxes(spatial_qkv, 2, 3), jnp.swapaxes(stream, 1, 2), sizes)
    mine, attended = lax.optimization_barrier((mine, attended))

    pieces = lax.all_gather(jnp.stack([each[:PAIR] for each in mine]), ("clip", "rank", "core"))
    same = jnp.stack([each[PAIR:] for each in mine])
    by_plane = [same] + [swap(same, ("clip", "rank"), plane, bit) for bit in range(1, plane)]
    arrived = lax.all_to_all(attended, "head", 0, 0)
    by_plane = jnp.stack(by_plane)
    by_core = swap(by_plane, "core", cores, 1)
    mixed = mix(info, by_plane, by_core, arrived, columns, ranks)
    mixed = around(mixed, ("rank", "core"), ranks)
    result = temporal(info, mixed, columns, pieces, sizes)
    arrived = [
        lax.ppermute(result[part * heads + step], ("outer", "clip", "head"), routes(step, part, sizes))
        for part in range(span // run) for step in range(heads)
    ]
    return jnp.swapaxes(place(info, arrived, sizes), 1, 2)


def solution(mesh):
    seq, heads = mesh.shape["seq"], mesh.shape["head"]

    def whole(spatial_qkv, stream, *rest):
        frames = spatial_qkv.shape[1] // seq
        ranks = FRAMES // frames
        clips_inner = SLICES // ranks
        shape = (seq // SLICES, clips_inner, ranks // 2, 2, heads)
        fine = Mesh(mesh.devices.reshape(shape), ("outer", "clip", "rank", "core", "head"))
        split = ("outer", "clip", "rank", "core")
        in_specs = (
            P(None, split, None, "head"),
            P(split, None, "head"),
            P("head", None),
            P(None, None, "head"),
            P("head", None),
            P(),
            P(),
            P(),
        )
        return jax.shard_map(
            functools.partial(on_device, shape), mesh=fine, in_specs=in_specs, out_specs=P(None, split, "head"),
            check_vma=False,
        )(spatial_qkv, stream, *rest)

    return whole
```

```python
import functools
import math

import jax
import jax.numpy as jnp
from jax import lax
from jax.experimental import pallas as pl
from jax.experimental.pallas import tpu as pltpu
from jax.sharding import Mesh
from jax.sharding import PartitionSpec as P

HEAD_DIM = 72
FRAMES = 8
PAIR = 2 * HEAD_DIM
KINDS = 3
SLICES = 8
EPS = 1e-6
F32 = jnp.float32
BF16 = jnp.bfloat16
MIB = 1024 * 1024


def flip(array):
    return jnp.swapaxes(array, 0, 1)


def tn(lhs, rhs):
    return lax.dot_general(lhs, rhs, (((0,), (0,)), ((), ())), preferred_element_type=F32)


def runs_of(chunk, rank, sizes):
    groups, ranks, heads, block, span, run = sizes
    starts = []
    for piece in range(span // run):
        place = chunk * span + piece * run
        starts.append((place // block * ranks + rank) * block + place % block)
    return starts


def spatial_kernel(sizes, info_ref, qkv_ref, stream_ref, out_ref, query_ref, key_ref, value_ref, part_ref):
    groups, ranks, heads, block, span, run = sizes
    chunk = pl.program_id(0)
    _, frames, width, tokens = qkv_ref.shape
    pairs = width // PAIR
    per_frame = tokens // heads
    scale = math.log2(math.e) / math.sqrt(HEAD_DIM)
    count = info_ref[0]

    @pl.when(chunk == 0)
    def arrange():
        for each in range(heads):
            for frame in range(frames):
                pieces = [
                    qkv_ref[0, frame, :, start:start + run]
                    for rank in range(ranks) for start in runs_of(each, rank, sizes)
                ]
                query_ref[each, frame] = jnp.concatenate(pieces, axis=1)
            pieces = [
                stream_ref[frame, :, start:start + run]
                for rank in range(ranks) for frame in range(frames) for start in runs_of(each, rank, sizes)
            ]
            out_ref[each, width:, :] = jnp.concatenate(pieces, axis=1)
        for frame in range(frames):
            key_ref[frame] = flip(qkv_ref[1, frame].astype(F32)).astype(BF16)
            for pair in range(pairs):
                value_ref[frame, pair, :PAIR, :] = qkv_ref[2, frame, pair * PAIR:(pair + 1) * PAIR, :]
                value_ref[frame, pair, PAIR:, :] = jnp.ones((value_ref.shape[2] - PAIR, tokens), BF16)

    def attend(keys, masked):
        for frame in range(frames):
            for head in range(2 * pairs):
                pair = head // 2
                low = (pair * PAIR) // 128 * 128
                high = min(-(-((pair + 1) * PAIR) // 128) * 128, width)
                row = lax.broadcasted_iota(jnp.int32, (high - low, per_frame), 0) + low
                mine = (row >= head * HEAD_DIM) & (row < (head + 1) * HEAD_DIM)
                query = jnp.where(mine, query_ref[chunk, frame, low:high, :], jnp.zeros((), BF16))
                scores = jnp.dot(key_ref[frame, :keys, low:high], query, preferred_element_type=F32)
                if masked:
                    token = lax.broadcasted_iota(jnp.int32, (keys, per_frame), 0)
                    scores = jnp.where(token < count, scores, -jnp.inf)
                highest = jnp.max(scores, axis=0, keepdims=True)
                raised = jnp.exp2(scores * scale - highest * scale).astype(BF16)
                summed = jnp.dot(value_ref[frame, pair, :, :keys], raised, preferred_element_type=F32)
                inside = head % 2 * HEAD_DIM
                result = summed[inside:inside + HEAD_DIM] / summed[PAIR:PAIR + 1]
                for rank in range(ranks):
                    lane = (rank * frames + frame) * span
                    part_ref[head * HEAD_DIM:(head + 1) * HEAD_DIM, lane:lane + span] = (
                        result[:, rank * span:(rank + 1) * span]
                    )

    half = tokens // 2

    @pl.when(count >= tokens)
    def whole():
        attend(tokens, False)

    @pl.when((count < tokens) & (count > half))
    def some():
        attend(tokens, True)

    @pl.when(count <= half)
    def few():
        attend(half, True)

    out_ref[chunk, :width, :] = part_ref[...].astype(BF16)


def spatial_attention(info, qkv, stream, sizes):
    groups, ranks, heads, block, span, run = sizes
    _, frames, width, tokens = qkv.shape
    rows = frames * tokens // heads
    pairs = width // PAIR
    vmem = pl.BlockSpec(memory_space=pltpu.VMEM)
    return pl.pallas_call(
        functools.partial(spatial_kernel, sizes),
        grid_spec=pltpu.PrefetchScalarGridSpec(
            num_scalar_prefetch=1,
            grid=(heads,),
            in_specs=[vmem, vmem],
            out_specs=vmem,
            scratch_shapes=[
                pltpu.VMEM((heads, frames, width, tokens // heads), BF16),
                pltpu.VMEM((frames, tokens, width), BF16),
                pltpu.VMEM((frames, pairs, PAIR + 16, tokens), BF16),
                pltpu.VMEM((width, rows), F32),
            ],
        ),
        out_shape=jax.ShapeDtypeStruct((heads, 2 * width, rows), BF16),
        compiler_params=pltpu.CompilerParams(vmem_limit_bytes=24 * MIB),
        cost_estimate=pl.CostEstimate(flops=28 * 10**9, bytes_accessed=5 * 10**6, transcendentals=8 * 10**6),
        name="spatial_attention",
    )(info, qkv, stream)


def mix_kernel(heads, ranks, info_ref, plane_ref, core_ref, gate_ref, rows_ref, *refs):
    out_refs, weight_ref, mixed_ref = refs[:-2], refs[-2], refs[-1]
    rank, me, core, member = info_ref[3], info_ref[4], info_ref[5], info_ref[6]
    members, _, strip, _ = plane_ref.shape
    width = rows_ref.shape[1] // 2
    half = weight_ref.shape[0] // (2 * heads)
    last = half // strip - 1
    for far, ref in enumerate((plane_ref, core_ref)):
        for other in range(members):
            whose = jnp.minimum(member ^ other, last)
            for step in range(heads):
                source = lax.rem(me - step + heads, heads)
                start = source * width + (core ^ far) * half + whose * strip
                weight_ref[pl.ds(pl.multiple_of(start, 16), strip), :] = ref[other, step]
    summed = None
    for source in range(heads):
        term = tn(weight_ref[source * width:(source + 1) * width, :], rows_ref[source, :width, :])
        summed = term if summed is None else summed + term
    for source in range(heads):
        here = slice(source * width, (source + 1) * width)
        mixed = rows_ref[source, width:, :].astype(F32) + gate_ref[here, 0:1] * summed[here]
        mixed_ref[here, :] = mixed.astype(BF16)
    lanes = mixed_ref.shape[1] // ranks
    for step in range(ranks):
        to = lax.rem(rank + step, ranks)
        out_refs[step][...] = mixed_ref[:, pl.ds(pl.multiple_of(to * lanes, lanes), lanes)]


def mix(info, by_plane, by_core, arrived, columns, ranks):
    heads, width, rows = arrived.shape
    width = width // 2
    features = by_plane.shape[3]
    vmem = pl.BlockSpec(memory_space=pltpu.VMEM)
    return pl.pallas_call(
        functools.partial(mix_kernel, heads, ranks),
        in_specs=[pl.BlockSpec(memory_space=pltpu.SMEM)] + [vmem] * 4,
        out_specs=[vmem] * ranks,
        out_shape=[jax.ShapeDtypeStruct((features, rows // ranks), BF16)] * ranks,
        scratch_shapes=[pltpu.VMEM((heads * width, features), BF16), pltpu.VMEM((features, rows), BF16)],
        compiler_params=pltpu.CompilerParams(vmem_limit_bytes=28 * MIB),
        cost_estimate=pl.CostEstimate(flops=5 * 10**9, bytes_accessed=4 * 10**6, transcendentals=0),
        name="mix",
    )(info, by_plane, by_core, columns, arrived)


def frame_at(place, rank, sizes):
    ranks = sizes[1]
    frames = FRAMES // ranks
    return lax.rem(rank - place // frames + ranks, ranks) * frames + place % frames


def temporal_kernel(sizes, info_ref, cols_ref, *refs):
    groups, ranks, heads, block, span, run = sizes
    kinds = KINDS + 1
    mixed_refs, refs = refs[:ranks], refs[ranks:]
    piece_refs, out_refs = refs[:2 * heads], refs[2 * heads:-5]
    normed_ref, attended_ref, result_ref, weight_ref, last_ref = refs[-5:]
    step = pl.program_id(0)
    features, lanes = mixed_refs[0].shape
    rows = ranks * lanes
    scale = 1.0 / math.sqrt(HEAD_DIM)
    frame_count = info_ref[1]
    rank_here = info_ref[3]

    @pl.when(step == 0)
    def norm():
        for rank in range(ranks):
            full = mixed_refs[rank][...].astype(F32)
            center = full - jnp.mean(full, axis=0, keepdims=True)
            variance = jnp.mean(center * center, axis=0, keepdims=True)
            normed = center * lax.rsqrt(variance + EPS)
            normed = normed * (1.0 + cols_ref[:, 2:3]) + cols_ref[:, 1:2]
            normed_ref[:, rank * lanes:(rank + 1) * lanes] = normed.astype(BF16)

    member = info_ref[6]
    here = pl.ds(pl.multiple_of(step * PAIR, PAIR), PAIR)
    for group in range(len(piece_refs) // 2):
        @pl.when(step // 2 == group)
        def take():
            for other in range(kinds):
                kind = member ^ other
                rows_to = pl.ds(pl.multiple_of(kind * PAIR, PAIR), PAIR)
                at = (other // 2, other % 2) if group % 2 == 0 else (other % 2, other // 2)
                weight_ref[rows_to, :] = piece_refs[2 * group + at[0]][at[1], step % 2]

    last_ref[here, :] = weight_ref[KINDS * PAIR:, :]
    projected = jnp.dot(weight_ref[:KINDS * PAIR, :], normed_ref[...], preferred_element_type=F32)
    frame = lax.broadcasted_iota(jnp.int32, (FRAMES, rows), 1) // span
    delta = lax.broadcasted_iota(jnp.int32, (FRAMES, rows), 0)
    key_frame = frame_at(lax.rem(frame - delta + FRAMES, FRAMES), rank_here, sizes)
    live = key_frame < frame_count

    def turned(array):
        return [array if d == 0 else pltpu.roll(array, d * span, 1) for d in range(FRAMES)]

    attended = []
    for head in range(2):
        query = projected[head * HEAD_DIM:(head + 1) * HEAD_DIM]
        key = projected[PAIR + head * HEAD_DIM:PAIR + (head + 1) * HEAD_DIM]
        value = projected[2 * PAIR + head * HEAD_DIM:2 * PAIR + (head + 1) * HEAD_DIM]
        scores = [jnp.sum(query * each, axis=0, keepdims=True) for each in turned(key)]
        scores = jnp.concatenate(scores, axis=0) * scale
        scores = jnp.where(live, scores, -jnp.inf)
        raised = jnp.exp(scores - jnp.max(scores, axis=0, keepdims=True))
        shares = raised / jnp.sum(raised, axis=0, keepdims=True)
        summed = None
        for d, each in enumerate(turned(value)):
            term = shares[d:d + 1] * each
            summed = term if summed is None else summed + term
        attended.append(summed)
    attended_ref[here, :] = jnp.concatenate(attended, axis=0).astype(BF16)

    @pl.when(step == pl.num_programs(0) - 1)
    def finish():
        width = features // heads
        clip, me, count = info_ref[2], info_ref[4], info_ref[0]
        total = tn(last_ref[...], attended_ref[...])
        for rank in range(ranks):
            lane = slice(rank * lanes, (rank + 1) * lanes)
            full = mixed_refs[rank][...].astype(F32) + cols_ref[:, 3:4] * total[:, lane]
            place = lax.broadcasted_iota(jnp.int32, (1, lanes), 1) + rank * lanes
            among = me * span + place % span
            token = (among // block * ranks + rank_here) * block + among % block
            valid = (frame_at(place // span, rank_here, sizes) < frame_count) & (token < count)
            result_ref[:, lane] = jnp.where(valid, full, 0.0).astype(BF16)
        parts = span // run
        share = max(heads // groups, 1)
        for part in range(parts):
            slot = lax.rem(part + parts - lax.rem(clip, parts), parts)
            turn = clip * share if parts == 1 else clip // parts
            for step_to in range(heads):
                to = lax.rem(me * (parts == 1) + step_to + turn, heads)
                rows_to = pl.ds(pl.multiple_of(to * width, width), width)

                def pick():
                    if parts == 1:
                        return result_ref[rows_to, :]
                    found = result_ref[rows_to, :]
                    return jnp.concatenate(
                        [found[:, f * span + part * run:f * span + (part + 1) * run] for f in range(FRAMES)], axis=1
                    )

                for each in range(parts):
                    @pl.when(slot == each)
                    def store():
                        out_refs[each * heads + step_to][...] = pick()


def temporal(info, mixed, columns, pieces, sizes):
    groups, ranks, heads, block, span, run = sizes
    features, lanes = mixed[0].shape
    rows = ranks * lanes
    kinds = KINDS + 1
    count = heads * (span // run)
    shape = (features // heads, FRAMES * run)

    return pl.pallas_call(
        functools.partial(temporal_kernel, sizes),
        grid_spec=pltpu.PrefetchScalarGridSpec(
            num_scalar_prefetch=1,
            grid=(2 * heads,),
            in_specs=[
                pl.BlockSpec(columns.shape, lambda s, info: (0, 0)),
            ] + [pl.BlockSpec(memory_space=pltpu.VMEM)] * (ranks + len(pieces)),
            out_specs=[pl.BlockSpec(shape, lambda s, info: (0, 0))] * count,
            scratch_shapes=[
                pltpu.VMEM((features, rows), BF16),
                pltpu.VMEM((features, rows), BF16),
                pltpu.VMEM((features, rows), BF16),
                pltpu.VMEM((kinds * PAIR, features), BF16),
                pltpu.VMEM((features, features), BF16),
            ],
        ),
        out_shape=[jax.ShapeDtypeStruct(shape, BF16)] * count,
        compiler_params=pltpu.CompilerParams(vmem_limit_bytes=24 * MIB),
        cost_estimate=pl.CostEstimate(flops=20 * 10**9, bytes_accessed=12 * 10**6, transcendentals=0),
        name="temporal",
    )(info, columns, *mixed, *pieces)


def place_kernel(sizes, info_ref, *refs):
    groups, ranks, heads, block, span, run = sizes
    parts = span // run
    share = block // run
    piece_refs, out_ref, held_ref = refs[:-2], refs[-2], refs[-1]
    clip, rank, me = info_ref[2], info_ref[3], info_ref[4]
    for part in range(parts):
        for step in range(heads):
            if parts == 1:
                source = lax.rem(me - step + heads + groups * heads - clip * share, heads)
            else:
                source = lax.rem(me - step + heads, heads) * parts + lax.rem(clip - part + parts, parts)
            held_ref[source] = piece_refs[part * heads + step][...]
    for group in range(groups):
        for at in range(FRAMES):
            pieces = [held_ref[group * share + e, :, at * run:(at + 1) * run] for e in range(share)]
            out_ref[group * FRAMES + frame_at(at, rank, sizes)] = jnp.concatenate(pieces, axis=1) if share > 1 else pieces[0]


def place(info, pieces, sizes):
    groups, ranks, heads, block, span, run = sizes
    width, lanes = pieces[0].shape
    vmem = pl.BlockSpec(memory_space=pltpu.VMEM)
    return pl.pallas_call(
        functools.partial(place_kernel, sizes),
        in_specs=[pl.BlockSpec(memory_space=pltpu.SMEM)] + [vmem] * len(pieces),
        out_specs=vmem,
        out_shape=jax.ShapeDtypeStruct((groups * FRAMES, width, block), BF16),
        scratch_shapes=[pltpu.VMEM((len(pieces), width, lanes), BF16)],
        compiler_params=pltpu.CompilerParams(vmem_limit_bytes=12 * MIB),
        name="place",
    )(info, *pieces)


def routes(step, part, sizes):
    groups, ranks, heads, block, span, run = sizes
    parts = span // run
    share = block // run
    pairs = []
    for clip in range(groups):
        for head in range(heads):
            if parts == 1:
                to = (head // share, (head + step + clip * share) % heads)
            else:
                to = (head * parts + (part + clip) % parts, (step + clip // parts) % heads)
            pairs.append((clip * heads + head, to[0] * heads + to[1]))
    return pairs


def on_device(
    shape, spatial_qkv, stream, out_spatial, qkv_temporal, out_temporal, modulation, tok_count, frame_count
):
    outer, clips_inner, rank_hi, cores, heads = shape
    groups = outer * clips_inner
    ranks = rank_hi * cores
    assert cores == 2 and clips_inner * rank_hi == KINDS + 1
    clip = lax.axis_index(("outer", "clip"))
    rank = lax.axis_index(("rank", "core"))
    core = lax.axis_index("core")
    head = lax.axis_index("head")
    member = lax.axis_index(("clip", "rank"))
    width = spatial_qkv.shape[3]
    features = out_spatial.shape[1]
    frames, tokens = stream.shape[:2]
    block = tokens // (groups * ranks)
    span = tokens // (ranks * heads)
    run = min(block, span)
    sizes = (groups, ranks, heads, block, span, run)

    def send(array, axis, size, step):
        return lax.ppermute(array, axis, [(i, (i + step) % size) for i in range(size)])

    def around(arrays, axis, size):
        return [arrays[0]] + [send(arrays[k], axis, size, k) for k in range(1, size)]

    def swap(array, axis, size, bit):
        return lax.ppermute(array, axis, [(i, i ^ bit) for i in range(size)])

    info = jnp.stack([tok_count[clip], frame_count[clip], clip, rank, head, core, member]).astype(jnp.int32)
    here = lax.dynamic_index_in_dim(modulation, clip, 0, keepdims=False)
    columns = here.T

    plane = clips_inner * rank_hi
    turned = jnp.swapaxes(qkv_temporal, 1, 2)
    weight = lax.dynamic_slice(turned, (jnp.minimum(member, KINDS - 1), core * PAIR, 0), (1, PAIR, features))[0]
    other = lax.dynamic_slice(out_temporal, (core * PAIR, 0), (PAIR, features))
    weight = jnp.where(member < KINDS, weight, other)
    half = width // cores
    strip = half // KINDS
    spatial = lax.dynamic_slice(
        out_spatial, (core * half + jnp.minimum(member, KINDS - 1) * strip, 0), (strip, features)
    )
    mine = jnp.concatenate([weight, spatial], axis=0)
    mine, info = lax.optimization_barrier((mine, info))
    mine = around([mine] * heads, "head", heads)
    attended = spatial_attention(info, jnp.swapaxes(spatial_qkv, 2, 3), jnp.swapaxes(stream, 1, 2), sizes)
    mine, attended = lax.optimization_barrier((mine, attended))

    arrived = lax.all_to_all(attended, "head", 0, 0)
    same = jnp.stack([each[PAIR:] for each in mine])
    by_plane = [same] + [swap(same, ("clip", "rank"), plane, bit) for bit in range(1, plane)]
    by_plane = jnp.stack(by_plane)
    by_core = swap(by_plane, "core", cores, 1)
    pieces = []
    for first, second, pair in ((1, 2, mine[:2]), (2, 1, mine[2:])):
        half = jnp.stack([each[:PAIR] for each in pair])
        half = jnp.stack([half, swap(half, ("clip", "rank"), plane, first)])
        pieces.append((half, swap(half, ("clip", "rank"), plane, second)))
    pieces = [each for group in pieces for each in group]
    crossed = [swap(each, "core", cores, 1) for each in pieces[::2]]
    mixed = mix(info, by_plane, by_core, arrived, columns, ranks)
    pieces, mixed = lax.optimization_barrier((pieces, mixed))
    mixed = around(mixed, ("rank", "core"), ranks)
    pieces += [crossed[0], swap(pieces[1], "core", cores, 1), crossed[1], swap(pieces[3], "core", cores, 1)]
    result = temporal(info, mixed, columns, pieces, sizes)
    arrived = [
        lax.ppermute(result[part * heads + step], ("outer", "clip", "head"), routes(step, part, sizes))
        for part in range(span // run) for step in range(heads)
    ]
    return jnp.swapaxes(place(info, arrived, sizes), 1, 2)


def solution(mesh):
    seq, heads = mesh.shape["seq"], mesh.shape["head"]

    def whole(spatial_qkv, stream, *rest):
        frames = spatial_qkv.shape[1] // seq
        ranks = FRAMES // frames
        clips_inner = SLICES // ranks
        shape = (seq // SLICES, clips_inner, ranks // 2, 2, heads)
        fine = Mesh(mesh.devices.reshape(shape), ("outer", "clip", "rank", "core", "head"))
        split = ("outer", "clip", "rank", "core")
        in_specs = (
            P(None, split, None, "head"),
            P(split, None, "head"),
            P("head", None),
            P(None, None, "head"),
            P("head", None),
            P(),
            P(),
            P(),
        )
        return jax.shard_map(
            functools.partial(on_device, shape), mesh=fine, in_specs=in_specs, out_specs=P(None, split, "head"),
            check_vma=False,
        )(spatial_qkv, stream, *rest)

    return whole
```

```python
import functools
import math

import jax
import jax.numpy as jnp
from jax import lax
from jax.experimental import pallas as pl
from jax.experimental.pallas import tpu as pltpu
from jax.sharding import Mesh
from jax.sharding import PartitionSpec as P

HEAD_DIM = 72
FRAMES = 8
PAIR = 2 * HEAD_DIM
KINDS = 3
SLICES = 8
EPS = 1e-6
F32 = jnp.float32
BF16 = jnp.bfloat16
MIB = 1024 * 1024


def flip(array):
    return jnp.swapaxes(array, 0, 1)


def tn(lhs, rhs):
    return lax.dot_general(lhs, rhs, (((0,), (0,)), ((), ())), preferred_element_type=F32)


def runs_of(chunk, rank, sizes):
    groups, ranks, heads, block, span, run = sizes
    starts = []
    for piece in range(span // run):
        place = chunk * span + piece * run
        starts.append((place // block * ranks + rank) * block + place % block)
    return starts


def arrange_kernel(sizes, qkv_ref, stream_ref, query_ref, key_ref, value_ref, rows_ref):
    groups, ranks, heads, block, span, run = sizes
    _, frames, width, tokens = qkv_ref.shape
    for each in range(heads):
        for frame in range(frames):
            pieces = [
                qkv_ref[0, frame, :, start:start + run]
                for rank in range(ranks) for start in runs_of(each, rank, sizes)
            ]
            gathered = jnp.concatenate(pieces, axis=1)
            for pair in range(width // PAIR):
                query_ref[each, frame, pair] = gathered[pair * PAIR:(pair + 1) * PAIR]
        pieces = [
            stream_ref[frame, :, start:start + run]
            for rank in range(ranks) for frame in range(frames) for start in runs_of(each, rank, sizes)
        ]
        rows_ref[each] = jnp.concatenate(pieces, axis=1)
    for frame in range(frames):
        for pair in range(width // PAIR):
            keys = qkv_ref[1, frame, pair * PAIR:(pair + 1) * PAIR, :]
            key_ref[frame, pair] = flip(keys.astype(F32)).astype(BF16)
            value_ref[frame, pair, :PAIR, :] = qkv_ref[2, frame, pair * PAIR:(pair + 1) * PAIR, :]
            value_ref[frame, pair, PAIR:, :] = jnp.ones((value_ref.shape[2] - PAIR, tokens), BF16)


def arrange(qkv, stream, sizes):
    heads = sizes[2]
    _, frames, width, tokens = qkv.shape
    shapes = [
        (heads, frames, width // PAIR, PAIR, tokens // heads),
        (frames, width // PAIR, tokens, PAIR),
        (frames, width // PAIR, PAIR + 16, tokens),
        (heads, width, frames * tokens // heads),
    ]
    vmem = pl.BlockSpec(memory_space=pltpu.VMEM)
    return pl.pallas_call(
        functools.partial(arrange_kernel, sizes),
        in_specs=[vmem] * 2,
        out_specs=[vmem] * len(shapes),
        out_shape=[jax.ShapeDtypeStruct(shape, BF16) for shape in shapes],
        compiler_params=pltpu.CompilerParams(vmem_limit_bytes=16 * MIB),
        cost_estimate=pl.CostEstimate(flops=6 * 10**9, bytes_accessed=5 * 10**6, transcendentals=0),
        name="arrange",
    )(qkv, stream)


def spatial_kernel(ranks, first, info_ref, query_ref, key_ref, value_ref, *refs):
    held_refs, out_ref, part_ref = refs[:-2], refs[-2], refs[-1]
    turn = pl.program_id(0)
    chunk = turn + first
    to = chunk if held_refs else turn
    _, frames, pairs, _, per_frame = query_ref.shape
    tokens = key_ref.shape[2]
    width = pairs * PAIR
    span = per_frame // ranks
    scale = math.log2(math.e) / math.sqrt(HEAD_DIM)
    count = info_ref[0]

    def attend(keys, masked):
        def of_pair(at, carry):
            frame, pair = at // pairs, at % pairs
            row = lax.broadcasted_iota(jnp.int32, (PAIR, per_frame), 0)
            queries = query_ref[chunk, frame, pair]
            for head in range(2):
                mine = (row >= head * HEAD_DIM) & (row < (head + 1) * HEAD_DIM)
                query = jnp.where(mine, queries, jnp.zeros((), BF16))
                scores = jnp.dot(key_ref[frame, pair, :keys, :], query, preferred_element_type=F32)
                if masked:
                    token = lax.broadcasted_iota(jnp.int32, (keys, per_frame), 0)
                    scores = jnp.where(token < count, scores, -jnp.inf)
                highest = jnp.max(scores, axis=0, keepdims=True)
                raised = jnp.exp2(scores * scale - highest * scale).astype(BF16)
                summed = jnp.dot(value_ref[frame, pair, :, :keys], raised, preferred_element_type=F32)
                inside = slice(head * HEAD_DIM, (head + 1) * HEAD_DIM)
                part_ref[frame, pair, inside, :] = summed[inside] / summed[PAIR:PAIR + 1]
            return carry

        lax.fori_loop(0, frames * pairs, of_pair, 0)

    half = tokens // 2

    @pl.when(count >= tokens)
    def whole():
        attend(tokens, False)

    @pl.when((count < tokens) & (count > half))
    def some():
        attend(tokens, True)

    @pl.when(count <= half)
    def few():
        attend(half, True)

    for pair in range(pairs):
        pieces = [
            part_ref[frame, pair, :, rank * span:(rank + 1) * span] for rank in range(ranks) for frame in range(frames)
        ]
        out_ref[to, pair * PAIR:(pair + 1) * PAIR, :] = jnp.concatenate(pieces, axis=1).astype(BF16)
    if held_refs:
        @pl.when(turn == 0)
        def join():
            out_ref[:first, :width, :] = held_refs[0][...]
            out_ref[:, width:, :] = held_refs[1][...]


def spatial_attention(info, queries, keys, values, ranks, first, count, *held):
    heads, frames, pairs, _, per_frame = queries.shape
    shape = (heads, 2 * pairs * PAIR, frames * per_frame) if held else (count, pairs * PAIR, frames * per_frame)
    vmem = pl.BlockSpec(memory_space=pltpu.VMEM)
    return pl.pallas_call(
        functools.partial(spatial_kernel, ranks, first),
        grid_spec=pltpu.PrefetchScalarGridSpec(
            num_scalar_prefetch=1,
            grid=(count,),
            in_specs=[vmem] * (3 + len(held)),
            out_specs=vmem,
            scratch_shapes=[pltpu.VMEM((frames, pairs, PAIR, per_frame), F32)],
        ),
        out_shape=jax.ShapeDtypeStruct(shape, BF16),
        compiler_params=pltpu.CompilerParams(vmem_limit_bytes=16 * MIB),
        cost_estimate=pl.CostEstimate(flops=14 * 10**9, bytes_accessed=5 * 10**6, transcendentals=4 * 10**6),
        name="spatial_attention",
    )(info, queries, keys, values, *held)


def strips_kernel(heads, info_ref, plane_ref, core_ref, out_ref):
    me, core, member = info_ref[4], info_ref[5], info_ref[6]
    members, _, strip, _ = plane_ref.shape
    width = out_ref.shape[0] // heads
    half = width // 2
    last = half // strip - 1
    for far, ref in enumerate((plane_ref, core_ref)):
        for other in range(members):
            whose = jnp.minimum(member ^ other, last)
            for step in range(heads):
                source = lax.rem(me - step + heads, heads)
                start = source * width + (core ^ far) * half + whose * strip
                out_ref[pl.ds(pl.multiple_of(start, 16), strip), :] = ref[other, step]


def strips_in_place(info, by_plane, by_core, width):
    heads, features = by_plane.shape[1], by_plane.shape[3]
    vmem = pl.BlockSpec(memory_space=pltpu.VMEM)
    return pl.pallas_call(
        functools.partial(strips_kernel, heads),
        in_specs=[pl.BlockSpec(memory_space=pltpu.SMEM)] + [vmem] * 2,
        out_specs=vmem,
        out_shape=jax.ShapeDtypeStruct((heads * width, features), BF16),
        compiler_params=pltpu.CompilerParams(vmem_limit_bytes=12 * MIB),
        cost_estimate=pl.CostEstimate(flops=2 * 10**9, bytes_accessed=5 * 10**6, transcendentals=0),
        name="strips_in_place",
    )(info, by_plane, by_core)


def mix_kernel(heads, ranks, info_ref, weight_ref, gate_ref, rows_ref, *refs):
    out_refs, mixed_ref = refs[:-1], refs[-1]
    rank = info_ref[3]
    width = rows_ref.shape[1] // 2
    summed = None
    for source in range(heads):
        term = tn(weight_ref[source * width:(source + 1) * width, :], rows_ref[source, :width, :])
        summed = term if summed is None else summed + term
    for source in range(heads):
        here = slice(source * width, (source + 1) * width)
        mixed = rows_ref[source, width:, :].astype(F32) + gate_ref[here, 0:1] * summed[here]
        mixed_ref[here, :] = mixed.astype(BF16)
    lanes = mixed_ref.shape[1] // ranks
    for step in range(ranks):
        to = lax.rem(rank + step, ranks)
        out_refs[step][...] = mixed_ref[:, pl.ds(pl.multiple_of(to * lanes, lanes), lanes)]


def mix(info, weight, arrived, columns, ranks):
    heads, width, rows = arrived.shape
    features = weight.shape[1]
    vmem = pl.BlockSpec(memory_space=pltpu.VMEM)
    return pl.pallas_call(
        functools.partial(mix_kernel, heads, ranks),
        in_specs=[pl.BlockSpec(memory_space=pltpu.SMEM)] + [vmem] * 3,
        out_specs=[vmem] * ranks,
        out_shape=[jax.ShapeDtypeStruct((features, rows // ranks), BF16)] * ranks,
        scratch_shapes=[pltpu.VMEM((features, rows), BF16)],
        compiler_params=pltpu.CompilerParams(vmem_limit_bytes=20 * MIB),
        cost_estimate=pl.CostEstimate(flops=4 * 10**9, bytes_accessed=4 * 10**6, transcendentals=0),
        name="mix",
    )(info, weight, columns, arrived)


def frame_at(place, rank, sizes):
    ranks = sizes[1]
    frames = FRAMES // ranks
    return lax.rem(rank - place // frames + ranks, ranks) * frames + place % frames


def pieces_kernel(info_ref, *refs):
    piece_refs, qkv_ref, out_ref = refs[:-2], refs[-2], refs[-1]
    member = info_ref[6]
    for group in range(len(piece_refs) // 2):
        for other in range(KINDS + 1):
            kind = member ^ other
            at = (other // 2, other % 2) if group % 2 == 0 else (other % 2, other // 2)
            ref = piece_refs[2 * group + at[0]]

            @pl.when(kind < KINDS)
            def projection():
                for head in range(2):
                    qkv_ref[2 * group + head, pl.ds(pl.multiple_of(kind * PAIR, 16), PAIR), :] = ref[at[1], head]

            @pl.when(kind == KINDS)
            def output():
                for head in range(2):
                    start = (2 * group + head) * PAIR
                    out_ref[start:start + PAIR, :] = ref[at[1], head]


def pieces_in_place(info, pieces):
    features = pieces[0].shape[3]
    count = features // PAIR
    vmem = pl.BlockSpec(memory_space=pltpu.VMEM)
    return pl.pallas_call(
        pieces_kernel,
        in_specs=[pl.BlockSpec(memory_space=pltpu.SMEM)] + [vmem] * len(pieces),
        out_specs=[vmem] * 2,
        out_shape=[
            jax.ShapeDtypeStruct((count, KINDS * PAIR, features), BF16),
            jax.ShapeDtypeStruct((features, features), BF16),
        ],
        compiler_params=pltpu.CompilerParams(vmem_limit_bytes=28 * MIB),
        cost_estimate=pl.CostEstimate(flops=3 * 10**9, bytes_accessed=20 * 10**6, transcendentals=0),
        name="pieces_in_place",
    )(info, *pieces)


def turned(array, span):
    lanes = array.shape[1]
    if 2 * span % 128 or span % 128 == 0:
        return [array if d == 0 else pltpu.roll(array, d * span, 1) for d in range(FRAMES)]
    odd = pltpu.roll(array, span, 1)
    found = []
    for d in range(FRAMES):
        base, shift = (odd, (d - 1) * span) if d % 2 else (array, d * span)
        whole = jnp.concatenate([base[:, lanes - shift:], base[:, :lanes - shift]], axis=1) if shift else base
        found.append(whole)
    return found


def temporal_kernel(sizes, info_ref, cols_ref, qkv_ref, last_ref, *refs):
    groups, ranks, heads, block, span, run = sizes
    mixed_refs, out_refs = refs[:ranks], refs[ranks:-3]
    normed_ref, attended_ref, result_ref = refs[-3:]
    step = pl.program_id(0)
    features, lanes = mixed_refs[0].shape
    rows = ranks * lanes
    scale = 1.0 / math.sqrt(HEAD_DIM)
    frame_count = info_ref[1]
    rank_here = info_ref[3]
    each_step = qkv_ref.shape[0] // pl.num_programs(0)

    @pl.when(step == 0)
    def norm():
        for rank in range(ranks):
            full = mixed_refs[rank][...].astype(F32)
            center = full - jnp.mean(full, axis=0, keepdims=True)
            variance = jnp.mean(center * center, axis=0, keepdims=True)
            normed = center * lax.rsqrt(variance + EPS)
            normed = normed * (1.0 + cols_ref[:, 2:3]) + cols_ref[:, 1:2]
            normed_ref[:, rank * lanes:(rank + 1) * lanes] = normed.astype(BF16)

    frame = lax.broadcasted_iota(jnp.int32, (FRAMES, rows), 1) // span
    delta = lax.broadcasted_iota(jnp.int32, (FRAMES, rows), 0)
    key_frame = frame_at(lax.rem(frame - delta + FRAMES, FRAMES), rank_here, sizes)
    live = key_frame < frame_count
    all_projected = [
        jnp.dot(qkv_ref[step * each_step + which], normed_ref[...], preferred_element_type=F32)
        for which in range(each_step)
    ]
    for which, projected in enumerate(all_projected):
        attended = []
        for head in range(2):
            query = projected[head * HEAD_DIM:(head + 1) * HEAD_DIM]
            key = projected[PAIR + head * HEAD_DIM:PAIR + (head + 1) * HEAD_DIM]
            value = projected[2 * PAIR + head * HEAD_DIM:2 * PAIR + (head + 1) * HEAD_DIM]
            scores = [jnp.sum(query * each, axis=0, keepdims=True) for each in turned(key, span)]
            scores = jnp.concatenate(scores, axis=0) * scale
            scores = jnp.where(live, scores, -jnp.inf)
            raised = jnp.exp(scores - jnp.max(scores, axis=0, keepdims=True))
            shares = raised / jnp.sum(raised, axis=0, keepdims=True)
            summed = None
            for d, each in enumerate(turned(value, span)):
                term = shares[d:d + 1] * each
                summed = term if summed is None else summed + term
            attended.append(summed)
        here = pl.ds(pl.multiple_of((step * each_step + which) * PAIR, PAIR), PAIR)
        attended_ref[here, :] = jnp.concatenate(attended, axis=0).astype(BF16)

    @pl.when(step == pl.num_programs(0) - 1)
    def finish():
        width = features // heads
        clip, me, count = info_ref[2], info_ref[4], info_ref[0]
        total = tn(last_ref[...], attended_ref[...])
        for rank in range(ranks):
            lane = slice(rank * lanes, (rank + 1) * lanes)
            full = mixed_refs[rank][...].astype(F32) + cols_ref[:, 3:4] * total[:, lane]
            place = lax.broadcasted_iota(jnp.int32, (1, lanes), 1) + rank * lanes
            among = me * span + place % span
            token = (among // block * ranks + rank_here) * block + among % block
            valid = (frame_at(place // span, rank_here, sizes) < frame_count) & (token < count)
            result_ref[:, lane] = jnp.where(valid, full, 0.0).astype(BF16)
        parts = span // run
        share = max(heads // groups, 1)
        for part in range(parts):
            slot = lax.rem(part + parts - lax.rem(clip, parts), parts)
            turn = clip * share if parts == 1 else clip // parts
            for step_to in range(heads):
                to = lax.rem(me * (parts == 1) + step_to + turn, heads)
                rows_to = pl.ds(pl.multiple_of(to * width, width), width)

                def pick():
                    if parts == 1:
                        return result_ref[rows_to, :]
                    found = result_ref[rows_to, :]
                    return jnp.concatenate(
                        [found[:, f * span + part * run:f * span + (part + 1) * run] for f in range(FRAMES)], axis=1
                    )

                for each in range(parts):
                    @pl.when(slot == each)
                    def store():
                        out_refs[each * heads + step_to][...] = pick()


def temporal(info, mixed, columns, weights, sizes):
    groups, ranks, heads, block, span, run = sizes
    features, lanes = mixed[0].shape
    rows = ranks * lanes
    count = heads * (span // run)
    shape = (features // heads, FRAMES * run)
    vmem = pl.BlockSpec(memory_space=pltpu.VMEM)
    return pl.pallas_call(
        functools.partial(temporal_kernel, sizes),
        grid_spec=pltpu.PrefetchScalarGridSpec(
            num_scalar_prefetch=1,
            grid=(heads,),
            in_specs=[vmem] * (3 + ranks),
            out_specs=[vmem] * count,
            scratch_shapes=[pltpu.VMEM((features, rows), BF16)] * 3,
        ),
        out_shape=[jax.ShapeDtypeStruct(shape, BF16)] * count,
        compiler_params=pltpu.CompilerParams(vmem_limit_bytes=20 * MIB),
        cost_estimate=pl.CostEstimate(flops=18 * 10**9, bytes_accessed=12 * 10**6, transcendentals=0),
        name="temporal",
    )(info, columns, *weights, *mixed)


def place_kernel(sizes, info_ref, *refs):
    groups, ranks, heads, block, span, run = sizes
    parts = span // run
    share = block // run
    piece_refs, out_ref, held_ref = refs[:-2], refs[-2], refs[-1]
    clip, rank, me = info_ref[2], info_ref[3], info_ref[4]
    for part in range(parts):
        for step in range(heads):
            if parts == 1:
                source = lax.rem(me - step + heads + groups * heads - clip * share, heads)
            else:
                source = lax.rem(me - step + heads, heads) * parts + lax.rem(clip - part + parts, parts)
            held_ref[source] = piece_refs[part * heads + step][...]
    for group in range(groups):
        for at in range(FRAMES):
            pieces = [held_ref[group * share + e, :, at * run:(at + 1) * run] for e in range(share)]
            out_ref[group * FRAMES + frame_at(at, rank, sizes)] = jnp.concatenate(pieces, axis=1) if share > 1 else pieces[0]


def place(info, pieces, sizes):
    groups, ranks, heads, block, span, run = sizes
    width, lanes = pieces[0].shape
    vmem = pl.BlockSpec(memory_space=pltpu.VMEM)
    return pl.pallas_call(
        functools.partial(place_kernel, sizes),
        in_specs=[pl.BlockSpec(memory_space=pltpu.SMEM)] + [vmem] * len(pieces),
        out_specs=vmem,
        out_shape=jax.ShapeDtypeStruct((groups * FRAMES, width, block), BF16),
        scratch_shapes=[pltpu.VMEM((len(pieces), width, lanes), BF16)],
        compiler_params=pltpu.CompilerParams(vmem_limit_bytes=12 * MIB),
        name="place",
    )(info, *pieces)


def routes(step, part, sizes):
    groups, ranks, heads, block, span, run = sizes
    parts = span // run
    share = block // run
    pairs = []
    for clip in range(groups):
        for head in range(heads):
            if parts == 1:
                to = (head // share, (head + step + clip * share) % heads)
            else:
                to = (head * parts + (part + clip) % parts, (step + clip // parts) % heads)
            pairs.append((clip * heads + head, to[0] * heads + to[1]))
    return pairs


def on_device(
    shape, spatial_qkv, stream, out_spatial, qkv_temporal, out_temporal, modulation, tok_count, frame_count
):
    outer, clips_inner, rank_hi, cores, heads = shape
    groups = outer * clips_inner
    ranks = rank_hi * cores
    assert cores == 2 and clips_inner * rank_hi == KINDS + 1
    clip = lax.axis_index(("outer", "clip"))
    rank = lax.axis_index(("rank", "core"))
    core = lax.axis_index("core")
    head = lax.axis_index("head")
    member = lax.axis_index(("clip", "rank"))
    width = spatial_qkv.shape[3]
    features = out_spatial.shape[1]
    frames, tokens = stream.shape[:2]
    block = tokens // (groups * ranks)
    span = tokens // (ranks * heads)
    run = min(block, span)
    sizes = (groups, ranks, heads, block, span, run)

    def send(array, axis, size, step):
        return lax.ppermute(array, axis, [(i, (i + step) % size) for i in range(size)])

    def around(arrays, axis, size):
        return [arrays[0]] + [send(arrays[k], axis, size, k) for k in range(1, size)]

    def swap(array, axis, size, bit):
        return lax.ppermute(array, axis, [(i, i ^ bit) for i in range(size)])

    info = jnp.stack([tok_count[clip], frame_count[clip], clip, rank, head, core, member]).astype(jnp.int32)
    here = lax.dynamic_index_in_dim(modulation, clip, 0, keepdims=False)
    columns = here.T

    plane = clips_inner * rank_hi
    turned = jnp.swapaxes(qkv_temporal, 1, 2)
    weight = lax.dynamic_slice(turned, (jnp.minimum(member, KINDS - 1), core * PAIR, 0), (1, PAIR, features))[0]
    other = lax.dynamic_slice(out_temporal, (core * PAIR, 0), (PAIR, features))
    weight = jnp.where(member < KINDS, weight, other)
    half = width // cores
    strip = half // KINDS
    spatial = lax.dynamic_slice(
        out_spatial, (core * half + jnp.minimum(member, KINDS - 1) * strip, 0), (strip, features)
    )
    spatial, info, weight = lax.optimization_barrier((spatial, info, weight))

    mine = around([weight] * heads, "head", heads)
    *arranged, rows = arrange(jnp.swapaxes(spatial_qkv, 2, 3), jnp.swapaxes(stream, 1, 2), sizes)
    early = spatial_attention(info, *arranged, ranks, 0, heads - 1)
    mine, early, spatial = lax.optimization_barrier((mine, early, spatial))

    first = [jnp.stack(pair) for pair in (mine[:2], mine[2:])]
    second = [swap(part, ("clip", "rank"), plane, bit) for part, bit in zip(first, (1, 2))]
    strips = around([spatial] * heads, "head", heads)
    first, info = lax.optimization_barrier((first, info))
    attended = spatial_attention(info, *arranged, ranks, heads - 1, 1, early, rows)
    first, second, strips, attended = lax.optimization_barrier((first, second, strips, attended))

    arrived = lax.all_to_all(attended, "head", 0, 0)
    pieces = []
    for near, far, bit in zip(first, second, (2, 1)):
        part = jnp.stack([near, far])
        pieces += [part, swap(part, ("clip", "rank"), plane, bit)]
    same = jnp.stack(strips)
    by_plane = jnp.stack([same] + [swap(same, ("clip", "rank"), plane, bit) for bit in range(1, plane)])
    strips = strips_in_place(info, by_plane, swap(by_plane, "core", cores, 1), width)
    pieces += [swap(each, "core", cores, 1) for each in pieces]
    arrived, strips = lax.optimization_barrier((arrived, strips))
    mixed = mix(info, strips, arrived, columns, ranks)
    mixed = around(mixed, ("rank", "core"), ranks)
    result = temporal(info, mixed, columns, pieces_in_place(info, pieces), sizes)
    arrived = [
        lax.ppermute(result[part * heads + step], ("outer", "clip", "head"), routes(step, part, sizes))
        for part in range(span // run) for step in range(heads)
    ]
    return jnp.swapaxes(place(info, arrived, sizes), 1, 2)


def solution(mesh):
    seq, heads = mesh.shape["seq"], mesh.shape["head"]

    def whole(spatial_qkv, stream, *rest):
        frames = spatial_qkv.shape[1] // seq
        ranks = FRAMES // frames
        clips_inner = SLICES // ranks
        shape = (seq // SLICES, clips_inner, ranks // 2, 2, heads)
        fine = Mesh(mesh.devices.reshape(shape), ("outer", "clip", "rank", "core", "head"))
        split = ("outer", "clip", "rank", "core")
        in_specs = (
            P(None, split, None, "head"),
            P(split, None, "head"),
            P("head", None),
            P(None, None, "head"),
            P("head", None),
            P(),
            P(),
            P(),
        )
        return jax.shard_map(
            functools.partial(on_device, shape), mesh=fine, in_specs=in_specs, out_specs=P(None, split, "head"),
            check_vma=False,
        )(spatial_qkv, stream, *rest)

    return whole
```

```python
import functools
import math

import jax
import jax.numpy as jnp
from jax import lax
from jax.experimental import pallas as pl
from jax.experimental.pallas import tpu as pltpu
from jax.sharding import Mesh
from jax.sharding import PartitionSpec as P

HEAD_DIM = 72
FRAMES = 8
PAIR = 2 * HEAD_DIM
KINDS = 3
SLICES = 8
EPS = 1e-6
F32 = jnp.float32
BF16 = jnp.bfloat16
MIB = 1024 * 1024


def flip(array):
    return jnp.swapaxes(array, 0, 1)


def tn(lhs, rhs):
    return lax.dot_general(lhs, rhs, (((0,), (0,)), ((), ())), preferred_element_type=F32)


def runs_of(chunk, rank, sizes):
    groups, ranks, heads, block, span, run = sizes
    starts = []
    for piece in range(span // run):
        place = chunk * span + piece * run
        starts.append((place // block * ranks + rank) * block + place % block)
    return starts


def arrange_kernel(sizes, qkv_ref, stream_ref, query_ref, key_ref, value_ref, rows_ref):
    groups, ranks, heads, block, span, run = sizes
    _, frames, width, tokens = qkv_ref.shape
    for each in range(heads):
        for frame in range(frames):
            pieces = [
                qkv_ref[0, frame, :, start:start + run]
                for rank in range(ranks) for start in runs_of(each, rank, sizes)
            ]
            gathered = jnp.concatenate(pieces, axis=1)
            for pair in range(width // PAIR):
                query_ref[each, frame, pair] = gathered[pair * PAIR:(pair + 1) * PAIR]
        pieces = [
            stream_ref[frame, :, start:start + run]
            for rank in range(ranks) for frame in range(frames) for start in runs_of(each, rank, sizes)
        ]
        rows_ref[each] = jnp.concatenate(pieces, axis=1)
    for frame in range(frames):
        for pair in range(width // PAIR):
            keys = qkv_ref[1, frame, pair * PAIR:(pair + 1) * PAIR, :]
            key_ref[frame, pair] = flip(keys.astype(F32)).astype(BF16)
            value_ref[frame, pair, :PAIR, :] = qkv_ref[2, frame, pair * PAIR:(pair + 1) * PAIR, :]
            value_ref[frame, pair, PAIR:, :] = jnp.ones((value_ref.shape[2] - PAIR, tokens), BF16)


def arrange(qkv, stream, sizes):
    heads = sizes[2]
    _, frames, width, tokens = qkv.shape
    shapes = [
        (heads, frames, width // PAIR, PAIR, tokens // heads),
        (frames, width // PAIR, tokens, PAIR),
        (frames, width // PAIR, PAIR + 16, tokens),
        (heads, width, frames * tokens // heads),
    ]
    vmem = pl.BlockSpec(memory_space=pltpu.VMEM)
    return pl.pallas_call(
        functools.partial(arrange_kernel, sizes),
        in_specs=[vmem] * 2,
        out_specs=[vmem] * len(shapes),
        out_shape=[jax.ShapeDtypeStruct(shape, BF16) for shape in shapes],
        compiler_params=pltpu.CompilerParams(vmem_limit_bytes=16 * MIB),
        cost_estimate=pl.CostEstimate(flops=6 * 10**9, bytes_accessed=5 * 10**6, transcendentals=0),
        name="arrange",
    )(qkv, stream)


def spatial_kernel(ranks, first, info_ref, query_ref, key_ref, value_ref, *refs):
    held_refs, out_ref, part_ref = refs[:-2], refs[-2], refs[-1]
    turn = pl.program_id(0)
    chunk = turn + first
    to = chunk if held_refs else turn
    _, frames, pairs, _, per_frame = query_ref.shape
    tokens = key_ref.shape[2]
    width = pairs * PAIR
    span = per_frame // ranks
    scale = math.log2(math.e) / math.sqrt(HEAD_DIM)
    count = info_ref[0]

    def attend(keys, masked):
        def of_pair(at, carry):
            frame, pair = at // pairs, at % pairs
            row = lax.broadcasted_iota(jnp.int32, (PAIR, per_frame), 0)
            queries = query_ref[chunk, frame, pair]
            for head in range(2):
                mine = (row >= head * HEAD_DIM) & (row < (head + 1) * HEAD_DIM)
                query = jnp.where(mine, queries, jnp.zeros((), BF16))
                scores = jnp.dot(key_ref[frame, pair, :keys, :], query, preferred_element_type=F32)
                if masked:
                    token = lax.broadcasted_iota(jnp.int32, (keys, per_frame), 0)
                    scores = jnp.where(token < count, scores, -jnp.inf)
                highest = jnp.max(scores, axis=0, keepdims=True)
                raised = jnp.exp2(scores * scale - highest * scale).astype(BF16)
                summed = jnp.dot(value_ref[frame, pair, :, :keys], raised, preferred_element_type=F32)
                inside = slice(head * HEAD_DIM, (head + 1) * HEAD_DIM)
                part_ref[frame, pair, inside, :] = summed[inside] / summed[PAIR:PAIR + 1]
            return carry

        lax.fori_loop(0, frames * pairs, of_pair, 0)

    half = tokens // 2

    @pl.when(count >= tokens)
    def whole():
        attend(tokens, False)

    @pl.when((count < tokens) & (count > half))
    def some():
        attend(tokens, True)

    @pl.when(count <= half)
    def few():
        attend(half, True)

    for pair in range(pairs):
        pieces = [
            part_ref[frame, pair, :, rank * span:(rank + 1) * span] for rank in range(ranks) for frame in range(frames)
        ]
        out_ref[to, pair * PAIR:(pair + 1) * PAIR, :] = jnp.concatenate(pieces, axis=1).astype(BF16)
    if held_refs:
        @pl.when(turn == 0)
        def join():
            out_ref[:first, :width, :] = held_refs[0][...]
            out_ref[:, width:, :] = held_refs[1][...]


def spatial_attention(info, queries, keys, values, ranks, first, count, *held):
    heads, frames, pairs, _, per_frame = queries.shape
    shape = (heads, 2 * pairs * PAIR, frames * per_frame) if held else (count, pairs * PAIR, frames * per_frame)
    vmem = pl.BlockSpec(memory_space=pltpu.VMEM)
    return pl.pallas_call(
        functools.partial(spatial_kernel, ranks, first),
        grid_spec=pltpu.PrefetchScalarGridSpec(
            num_scalar_prefetch=1,
            grid=(count,),
            in_specs=[vmem] * (3 + len(held)),
            out_specs=vmem,
            scratch_shapes=[pltpu.VMEM((frames, pairs, PAIR, per_frame), F32)],
        ),
        out_shape=jax.ShapeDtypeStruct(shape, BF16),
        compiler_params=pltpu.CompilerParams(vmem_limit_bytes=16 * MIB),
        cost_estimate=pl.CostEstimate(flops=14 * 10**9, bytes_accessed=5 * 10**6, transcendentals=4 * 10**6),
        name="spatial_attention",
    )(info, queries, keys, values, *held)


def mix_kernel(heads, ranks, info_ref, plane_ref, core_ref, gates_ref, rows_ref, *refs):
    out_refs, weight_ref, mixed_ref = refs[:-2], refs[-2], refs[-1]
    rank, me, core, member = info_ref[3], info_ref[4], info_ref[5], info_ref[6]
    members, _, strip, _ = plane_ref.shape
    width = rows_ref.shape[1] // 2
    half = width // 2
    last = half // strip - 1
    gate = flip(gates_ref[...])[:, 0:1]
    for far, ref in enumerate((plane_ref, core_ref)):
        for other in range(members):
            whose = jnp.minimum(member ^ other, last)
            for step in range(heads):
                source = lax.rem(me - step + heads, heads)
                start = source * width + (core ^ far) * half + whose * strip
                weight_ref[pl.ds(pl.multiple_of(start, 16), strip), :] = ref[other, step]
    summed = None
    for source in range(heads):
        term = tn(weight_ref[source * width:(source + 1) * width, :], rows_ref[source, :width, :])
        summed = term if summed is None else summed + term
    for source in range(heads):
        here = slice(source * width, (source + 1) * width)
        mixed = rows_ref[source, width:, :].astype(F32) + gate[here] * summed[here]
        mixed_ref[here, :] = mixed.astype(BF16)
    lanes = mixed_ref.shape[1] // ranks
    for step in range(ranks):
        to = lax.rem(rank + step, ranks)
        out_refs[step][...] = mixed_ref[:, pl.ds(pl.multiple_of(to * lanes, lanes), lanes)]


def mix(info, by_plane, by_core, arrived, gates, ranks):
    heads, width, rows = arrived.shape
    features = by_plane.shape[3]
    vmem = pl.BlockSpec(memory_space=pltpu.VMEM)
    return pl.pallas_call(
        functools.partial(mix_kernel, heads, ranks),
        in_specs=[pl.BlockSpec(memory_space=pltpu.SMEM)] + [vmem] * 4,
        out_specs=[vmem] * ranks,
        out_shape=[jax.ShapeDtypeStruct((features, rows // ranks), BF16)] * ranks,
        scratch_shapes=[pltpu.VMEM((features, features), BF16), pltpu.VMEM((features, rows), BF16)],
        compiler_params=pltpu.CompilerParams(vmem_limit_bytes=20 * MIB),
        cost_estimate=pl.CostEstimate(flops=4 * 10**9, bytes_accessed=4 * 10**6, transcendentals=0),
        name="mix",
    )(info, by_plane, by_core, gates, arrived)


def frame_at(place, rank, sizes):
    ranks = sizes[1]
    frames = FRAMES // ranks
    return lax.rem(rank - place // frames + ranks, ranks) * frames + place % frames


def pieces_kernel(info_ref, *refs):
    piece_refs, qkv_ref, out_ref = refs[:-2], refs[-2], refs[-1]
    member = info_ref[6]
    for group in range(len(piece_refs) // 2):
        for other in range(KINDS + 1):
            kind = member ^ other
            at = (other // 2, other % 2) if group % 2 == 0 else (other % 2, other // 2)
            ref = piece_refs[2 * group + at[0]]

            @pl.when(kind < KINDS)
            def projection():
                for head in range(2):
                    qkv_ref[2 * group + head, pl.ds(pl.multiple_of(kind * PAIR, 16), PAIR), :] = ref[at[1], head]

            @pl.when(kind == KINDS)
            def output():
                for head in range(2):
                    start = (2 * group + head) * PAIR
                    out_ref[start:start + PAIR, :] = ref[at[1], head]


def pieces_in_place(info, pieces):
    features = pieces[0].shape[3]
    count = features // PAIR
    vmem = pl.BlockSpec(memory_space=pltpu.VMEM)
    return pl.pallas_call(
        pieces_kernel,
        in_specs=[pl.BlockSpec(memory_space=pltpu.SMEM)] + [vmem] * len(pieces),
        out_specs=[vmem] * 2,
        out_shape=[
            jax.ShapeDtypeStruct((count, KINDS * PAIR, features), BF16),
            jax.ShapeDtypeStruct((features, features), BF16),
        ],
        compiler_params=pltpu.CompilerParams(vmem_limit_bytes=28 * MIB),
        cost_estimate=pl.CostEstimate(flops=3 * 10**9, bytes_accessed=20 * 10**6, transcendentals=0),
        name="pieces_in_place",
    )(info, *pieces)


def turned(array, span):
    lanes = array.shape[1]
    if 2 * span % 128 or span % 128 == 0:
        return [array if d == 0 else pltpu.roll(array, d * span, 1) for d in range(FRAMES)]
    odd = pltpu.roll(array, span, 1)
    found = []
    for d in range(FRAMES):
        base, shift = (odd, (d - 1) * span) if d % 2 else (array, d * span)
        whole = jnp.concatenate([base[:, lanes - shift:], base[:, :lanes - shift]], axis=1) if shift else base
        found.append(whole)
    return found


def temporal_kernel(sizes, info_ref, gates_ref, qkv_ref, last_ref, *refs):
    groups, ranks, heads, block, span, run = sizes
    mixed_refs, out_refs = refs[:ranks], refs[ranks:-3]
    normed_ref, attended_ref, result_ref = refs[-3:]
    step = pl.program_id(0)
    features, lanes = mixed_refs[0].shape
    rows = ranks * lanes
    scale = 1.0 / math.sqrt(HEAD_DIM)
    frame_count = info_ref[1]
    rank_here = info_ref[3]
    each_step = qkv_ref.shape[0] // pl.num_programs(0)

    @pl.when(step == 0)
    def norm():
        columns = flip(gates_ref[...])
        for rank in range(ranks):
            full = mixed_refs[rank][...].astype(F32)
            center = full - jnp.mean(full, axis=0, keepdims=True)
            variance = jnp.mean(center * center, axis=0, keepdims=True)
            normed = center * lax.rsqrt(variance + EPS)
            normed = normed * (1.0 + columns[:, 2:3]) + columns[:, 1:2]
            normed_ref[:, rank * lanes:(rank + 1) * lanes] = normed.astype(BF16)

    frame = lax.broadcasted_iota(jnp.int32, (FRAMES, rows), 1) // span
    delta = lax.broadcasted_iota(jnp.int32, (FRAMES, rows), 0)
    key_frame = frame_at(lax.rem(frame - delta + FRAMES, FRAMES), rank_here, sizes)
    live = key_frame < frame_count
    all_projected = [
        jnp.dot(qkv_ref[step * each_step + which], normed_ref[...], preferred_element_type=F32)
        for which in range(each_step)
    ]
    for which, projected in enumerate(all_projected):
        attended = []
        for head in range(2):
            query = projected[head * HEAD_DIM:(head + 1) * HEAD_DIM]
            key = projected[PAIR + head * HEAD_DIM:PAIR + (head + 1) * HEAD_DIM]
            value = projected[2 * PAIR + head * HEAD_DIM:2 * PAIR + (head + 1) * HEAD_DIM]
            scores = [jnp.sum(query * each, axis=0, keepdims=True) for each in turned(key, span)]
            scores = jnp.concatenate(scores, axis=0) * scale
            scores = jnp.where(live, scores, -jnp.inf)
            raised = jnp.exp(scores - jnp.max(scores, axis=0, keepdims=True))
            shares = raised / jnp.sum(raised, axis=0, keepdims=True)
            summed = None
            for d, each in enumerate(turned(value, span)):
                term = shares[d:d + 1] * each
                summed = term if summed is None else summed + term
            attended.append(summed)
        here = pl.ds(pl.multiple_of((step * each_step + which) * PAIR, PAIR), PAIR)
        attended_ref[here, :] = jnp.concatenate(attended, axis=0).astype(BF16)

    @pl.when(step == pl.num_programs(0) - 1)
    def finish():
        width = features // heads
        clip, me, count = info_ref[2], info_ref[4], info_ref[0]
        gate = flip(gates_ref[...])[:, 3:4]
        total = tn(last_ref[...], attended_ref[...])
        for rank in range(ranks):
            lane = slice(rank * lanes, (rank + 1) * lanes)
            full = mixed_refs[rank][...].astype(F32) + gate * total[:, lane]
            place = lax.broadcasted_iota(jnp.int32, (1, lanes), 1) + rank * lanes
            among = me * span + place % span
            token = (among // block * ranks + rank_here) * block + among % block
            valid = (frame_at(place // span, rank_here, sizes) < frame_count) & (token < count)
            result_ref[:, lane] = jnp.where(valid, full, 0.0).astype(BF16)
        parts = span // run
        share = max(heads // groups, 1)
        for part in range(parts):
            slot = lax.rem(part + parts - lax.rem(clip, parts), parts)
            turn = clip * share if parts == 1 else clip // parts
            for step_to in range(heads):
                to = lax.rem(me * (parts == 1) + step_to + turn, heads)
                rows_to = pl.ds(pl.multiple_of(to * width, width), width)

                def pick():
                    if parts == 1:
                        return result_ref[rows_to, :]
                    found = result_ref[rows_to, :]
                    return jnp.concatenate(
                        [found[:, f * span + part * run:f * span + (part + 1) * run] for f in range(FRAMES)], axis=1
                    )

                for each in range(parts):
                    @pl.when(slot == each)
                    def store():
                        out_refs[each * heads + step_to][...] = pick()


def temporal(info, mixed, gates, weights, sizes):
    groups, ranks, heads, block, span, run = sizes
    features, lanes = mixed[0].shape
    rows = ranks * lanes
    count = heads * (span // run)
    shape = (features // heads, FRAMES * run)
    vmem = pl.BlockSpec(memory_space=pltpu.VMEM)
    return pl.pallas_call(
        functools.partial(temporal_kernel, sizes),
        grid_spec=pltpu.PrefetchScalarGridSpec(
            num_scalar_prefetch=1,
            grid=(heads,),
            in_specs=[vmem] * (3 + ranks),
            out_specs=[vmem] * count,
            scratch_shapes=[pltpu.VMEM((features, rows), BF16)] * 3,
        ),
        out_shape=[jax.ShapeDtypeStruct(shape, BF16)] * count,
        compiler_params=pltpu.CompilerParams(vmem_limit_bytes=20 * MIB),
        cost_estimate=pl.CostEstimate(flops=18 * 10**9, bytes_accessed=12 * 10**6, transcendentals=0),
        name="temporal",
    )(info, gates, *weights, *mixed)


def place_kernel(sizes, info_ref, *refs):
    groups, ranks, heads, block, span, run = sizes
    parts = span // run
    share = block // run
    piece_refs, out_ref, held_ref = refs[:-2], refs[-2], refs[-1]
    clip, rank, me = info_ref[2], info_ref[3], info_ref[4]
    for part in range(parts):
        for step in range(heads):
            if parts == 1:
                source = lax.rem(me - step + heads + groups * heads - clip * share, heads)
            else:
                source = lax.rem(me - step + heads, heads) * parts + lax.rem(clip - part + parts, parts)
            held_ref[source] = piece_refs[part * heads + step][...]
    for group in range(groups):
        for at in range(FRAMES):
            pieces = [held_ref[group * share + e, :, at * run:(at + 1) * run] for e in range(share)]
            out_ref[group * FRAMES + frame_at(at, rank, sizes)] = jnp.concatenate(pieces, axis=1) if share > 1 else pieces[0]


def place(info, pieces, sizes):
    groups, ranks, heads, block, span, run = sizes
    width, lanes = pieces[0].shape
    vmem = pl.BlockSpec(memory_space=pltpu.VMEM)
    return pl.pallas_call(
        functools.partial(place_kernel, sizes),
        in_specs=[pl.BlockSpec(memory_space=pltpu.SMEM)] + [vmem] * len(pieces),
        out_specs=vmem,
        out_shape=jax.ShapeDtypeStruct((groups * FRAMES, width, block), BF16),
        scratch_shapes=[pltpu.VMEM((len(pieces), width, lanes), BF16)],
        compiler_params=pltpu.CompilerParams(vmem_limit_bytes=12 * MIB),
        name="place",
    )(info, *pieces)


def routes(step, part, sizes):
    groups, ranks, heads, block, span, run = sizes
    parts = span // run
    share = block // run
    pairs = []
    for clip in range(groups):
        for head in range(heads):
            if parts == 1:
                to = (head // share, (head + step + clip * share) % heads)
            else:
                to = (head * parts + (part + clip) % parts, (step + clip // parts) % heads)
            pairs.append((clip * heads + head, to[0] * heads + to[1]))
    return pairs


def on_device(
    shape, spatial_qkv, stream, out_spatial, qkv_temporal, out_temporal, modulation, tok_count, frame_count
):
    outer, clips_inner, rank_hi, cores, heads = shape
    groups = outer * clips_inner
    ranks = rank_hi * cores
    assert cores == 2 and clips_inner * rank_hi == KINDS + 1
    clip = lax.axis_index(("outer", "clip"))
    rank = lax.axis_index(("rank", "core"))
    core = lax.axis_index("core")
    head = lax.axis_index("head")
    member = lax.axis_index(("clip", "rank"))
    width = spatial_qkv.shape[3]
    features = out_spatial.shape[1]
    frames, tokens = stream.shape[:2]
    block = tokens // (groups * ranks)
    span = tokens // (ranks * heads)
    run = min(block, span)
    sizes = (groups, ranks, heads, block, span, run)

    def send(array, axis, size, step):
        return lax.ppermute(array, axis, [(i, (i + step) % size) for i in range(size)])

    def around(arrays, axis, size):
        return [arrays[0]] + [send(arrays[k], axis, size, k) for k in range(1, size)]

    def swap(array, axis, size, bit):
        return lax.ppermute(array, axis, [(i, i ^ bit) for i in range(size)])

    info = jnp.stack([tok_count[clip], frame_count[clip], clip, rank, head, core, member]).astype(jnp.int32)
    here = lax.dynamic_index_in_dim(modulation, clip, 0, keepdims=False)
    gates = jnp.concatenate([here, here], axis=0)

    plane = clips_inner * rank_hi
    turned = jnp.swapaxes(qkv_temporal, 1, 2)
    weight = lax.dynamic_slice(turned, (jnp.minimum(member, KINDS - 1), core * PAIR, 0), (1, PAIR, features))[0]
    other = lax.dynamic_slice(out_temporal, (core * PAIR, 0), (PAIR, features))
    weight = jnp.where(member < KINDS, weight, other)
    half = width // cores
    strip = half // KINDS
    spatial = lax.dynamic_slice(
        out_spatial, (core * half + jnp.minimum(member, KINDS - 1) * strip, 0), (strip, features)
    )
    spatial, info, weight = lax.optimization_barrier((spatial, info, weight))

    mine = around([weight] * heads, "head", heads)
    *arranged, rows = arrange(jnp.swapaxes(spatial_qkv, 2, 3), jnp.swapaxes(stream, 1, 2), sizes)
    early = spatial_attention(info, *arranged, ranks, 0, heads - 1)
    mine, early, spatial = lax.optimization_barrier((mine, early, spatial))

    first = [jnp.stack(pair) for pair in (mine[:2], mine[2:])]
    second = [swap(part, ("clip", "rank"), plane, bit) for part, bit in zip(first, (1, 2))]
    strips = around([spatial] * heads, "head", heads)
    first, info = lax.optimization_barrier((first, info))
    attended = spatial_attention(info, *arranged, ranks, heads - 1, 1, early, rows)
    first, second, strips, attended = lax.optimization_barrier((first, second, strips, attended))

    arrived = lax.all_to_all(attended, "head", 0, 0)
    pieces = []
    for near, far, bit in zip(first, second, (2, 1)):
        part = jnp.stack([near, far])
        pieces += [part, swap(part, ("clip", "rank"), plane, bit)]
    same = jnp.stack(strips)
    by_plane = jnp.stack([same] + [swap(same, ("clip", "rank"), plane, bit) for bit in range(1, plane)])
    by_core = swap(by_plane, "core", cores, 1)
    pieces += [swap(each, "core", cores, 1) for each in pieces]
    mixed = mix(info, by_plane, by_core, arrived, gates, ranks)
    mixed = around(mixed, ("rank", "core"), ranks)
    result = temporal(info, mixed, gates, pieces_in_place(info, pieces), sizes)
    arrived = [
        lax.ppermute(result[part * heads + step], ("outer", "clip", "head"), routes(step, part, sizes))
        for part in range(span // run) for step in range(heads)
    ]
    return jnp.swapaxes(place(info, arrived, sizes), 1, 2)


def solution(mesh):
    seq, heads = mesh.shape["seq"], mesh.shape["head"]

    def whole(spatial_qkv, stream, *rest):
        frames = spatial_qkv.shape[1] // seq
        ranks = FRAMES // frames
        clips_inner = SLICES // ranks
        shape = (seq // SLICES, clips_inner, ranks // 2, 2, heads)
        fine = Mesh(mesh.devices.reshape(shape), ("outer", "clip", "rank", "core", "head"))
        split = ("outer", "clip", "rank", "core")
        in_specs = (
            P(None, split, None, "head"),
            P(split, None, "head"),
            P("head", None),
            P(None, None, "head"),
            P("head", None),
            P(),
            P(),
            P(),
        )
        return jax.shard_map(
            functools.partial(on_device, shape), mesh=fine, in_specs=in_specs, out_specs=P(None, split, "head"),
            check_vma=False,
        )(spatial_qkv, stream, *rest)

    return whole
```

```python
import functools
import math

import jax
import jax.numpy as jnp
from jax import lax
from jax.experimental import pallas as pl
from jax.experimental.pallas import tpu as pltpu
from jax.sharding import Mesh
from jax.sharding import PartitionSpec as P

HEAD_DIM = 72
FRAMES = 8
PAIR = 2 * HEAD_DIM
KINDS = 3
SLICES = 8
EPS = 1e-6
F32 = jnp.float32
BF16 = jnp.bfloat16
MIB = 1024 * 1024


def flip(array):
    return jnp.swapaxes(array, 0, 1)


def tn(lhs, rhs):
    return lax.dot_general(lhs, rhs, (((0,), (0,)), ((), ())), preferred_element_type=F32)


def runs_of(chunk, rank, sizes):
    groups, ranks, heads, block, span, run = sizes
    starts = []
    for piece in range(span // run):
        place = chunk * span + piece * run
        starts.append((place // block * ranks + rank) * block + place % block)
    return starts


def arrange_kernel(sizes, qkv_ref, stream_ref, query_ref, key_ref, value_ref, rows_ref):
    groups, ranks, heads, block, span, run = sizes
    _, frames, width, tokens = qkv_ref.shape
    for each in range(heads):
        for frame in range(frames):
            pieces = [
                qkv_ref[0, frame, :, start:start + run]
                for rank in range(ranks) for start in runs_of(each, rank, sizes)
            ]
            gathered = jnp.concatenate(pieces, axis=1)
            for pair in range(width // PAIR):
                query_ref[each, frame, pair] = gathered[pair * PAIR:(pair + 1) * PAIR]
        pieces = [
            stream_ref[frame, :, start:start + run]
            for rank in range(ranks) for frame in range(frames) for start in runs_of(each, rank, sizes)
        ]
        rows_ref[each] = jnp.concatenate(pieces, axis=1)
    for frame in range(frames):
        for pair in range(width // PAIR):
            keys = qkv_ref[1, frame, pair * PAIR:(pair + 1) * PAIR, :]
            key_ref[frame, pair] = flip(keys.astype(F32)).astype(BF16)
            value_ref[frame, pair, :PAIR, :] = qkv_ref[2, frame, pair * PAIR:(pair + 1) * PAIR, :]
            value_ref[frame, pair, PAIR:, :] = jnp.ones((value_ref.shape[2] - PAIR, tokens), BF16)


def arrange(qkv, stream, sizes):
    heads = sizes[2]
    _, frames, width, tokens = qkv.shape
    shapes = [
        (heads, frames, width // PAIR, PAIR, tokens // heads),
        (frames, width // PAIR, tokens, PAIR),
        (frames, width // PAIR, PAIR + 16, tokens),
        (heads, width, frames * tokens // heads),
    ]
    vmem = pl.BlockSpec(memory_space=pltpu.VMEM)
    return pl.pallas_call(
        functools.partial(arrange_kernel, sizes),
        in_specs=[vmem] * 2,
        out_specs=[vmem] * len(shapes),
        out_shape=[jax.ShapeDtypeStruct(shape, BF16) for shape in shapes],
        compiler_params=pltpu.CompilerParams(vmem_limit_bytes=16 * MIB),
        cost_estimate=pl.CostEstimate(flops=6 * 10**9, bytes_accessed=5 * 10**6, transcendentals=0),
        name="arrange",
    )(qkv, stream)


def spatial_kernel(ranks, first, info_ref, query_ref, key_ref, value_ref, *refs):
    held_refs, out_ref, part_ref = refs[:-2], refs[-2], refs[-1]
    turn = pl.program_id(0)
    chunk = turn + first
    to = chunk if held_refs else turn
    _, frames, pairs, _, per_frame = query_ref.shape
    tokens = key_ref.shape[2]
    width = pairs * PAIR
    span = per_frame // ranks
    scale = math.log2(math.e) / math.sqrt(HEAD_DIM)
    count = info_ref[0]

    def attend(keys, masked):
        def of_pair(at, carry):
            frame, pair = at // pairs, at % pairs
            row = lax.broadcasted_iota(jnp.int32, (PAIR, per_frame), 0)
            queries = query_ref[chunk, frame, pair]
            for head in range(2):
                mine = (row >= head * HEAD_DIM) & (row < (head + 1) * HEAD_DIM)
                query = jnp.where(mine, queries, jnp.zeros((), BF16))
                scores = jnp.dot(key_ref[frame, pair, :keys, :], query, preferred_element_type=F32)
                if masked:
                    token = lax.broadcasted_iota(jnp.int32, (keys, per_frame), 0)
                    scores = jnp.where(token < count, scores, -jnp.inf)
                highest = jnp.max(scores, axis=0, keepdims=True)
                raised = jnp.exp2(scores * scale - highest * scale).astype(BF16)
                summed = jnp.dot(value_ref[frame, pair, :, :keys], raised, preferred_element_type=F32)
                inside = slice(head * HEAD_DIM, (head + 1) * HEAD_DIM)
                part_ref[frame, pair, inside, :] = summed[inside] / summed[PAIR:PAIR + 1]
            return carry

        lax.fori_loop(0, frames * pairs, of_pair, 0)

    half = tokens // 2

    @pl.when(count >= tokens)
    def whole():
        attend(tokens, False)

    @pl.when((count < tokens) & (count > half))
    def some():
        attend(tokens, True)

    @pl.when(count <= half)
    def few():
        attend(half, True)

    for pair in range(pairs):
        pieces = [
            part_ref[frame, pair, :, rank * span:(rank + 1) * span] for rank in range(ranks) for frame in range(frames)
        ]
        out_ref[to, pair * PAIR:(pair + 1) * PAIR, :] = jnp.concatenate(pieces, axis=1).astype(BF16)
    if held_refs:
        @pl.when(turn == 0)
        def join():
            out_ref[:first, :width, :] = held_refs[0][...]
            out_ref[:, width:, :] = held_refs[1][...]


def spatial_attention(info, queries, keys, values, ranks, first, count, *held):
    heads, frames, pairs, _, per_frame = queries.shape
    shape = (heads, 2 * pairs * PAIR, frames * per_frame) if held else (count, pairs * PAIR, frames * per_frame)
    vmem = pl.BlockSpec(memory_space=pltpu.VMEM)
    return pl.pallas_call(
        functools.partial(spatial_kernel, ranks, first),
        grid_spec=pltpu.PrefetchScalarGridSpec(
            num_scalar_prefetch=1,
            grid=(count,),
            in_specs=[vmem] * (3 + len(held)),
            out_specs=vmem,
            scratch_shapes=[pltpu.VMEM((frames, pairs, PAIR, per_frame), F32)],
        ),
        out_shape=jax.ShapeDtypeStruct(shape, BF16),
        compiler_params=pltpu.CompilerParams(vmem_limit_bytes=16 * MIB),
        cost_estimate=pl.CostEstimate(flops=14 * 10**9, bytes_accessed=5 * 10**6, transcendentals=4 * 10**6),
        name="spatial_attention",
    )(info, queries, keys, values, *held)


def mix_kernel(heads, ranks, info_ref, plane_ref, core_ref, gates_ref, rows_ref, *refs):
    out_refs, weight_ref, mixed_ref = refs[:-2], refs[-2], refs[-1]
    rank, me, core, member = info_ref[3], info_ref[4], info_ref[5], info_ref[6]
    members, _, strip, _ = plane_ref.shape
    width = rows_ref.shape[1] // 2
    half = width // 2
    last = half // strip - 1
    gate = flip(gates_ref[...])[:, 0:1]
    for far, ref in enumerate((plane_ref, core_ref)):
        for other in range(members):
            whose = jnp.minimum(member ^ other, last)
            for step in range(heads):
                source = lax.rem(me - step + heads, heads)
                start = source * width + (core ^ far) * half + whose * strip
                weight_ref[pl.ds(pl.multiple_of(start, 16), strip), :] = ref[other, step]
    summed = None
    for source in range(heads):
        term = tn(weight_ref[source * width:(source + 1) * width, :], rows_ref[source, :width, :])
        summed = term if summed is None else summed + term
    for source in range(heads):
        here = slice(source * width, (source + 1) * width)
        mixed = rows_ref[source, width:, :].astype(F32) + gate[here] * summed[here]
        mixed_ref[here, :] = mixed.astype(BF16)
    lanes = mixed_ref.shape[1] // ranks
    for step in range(ranks):
        to = lax.rem(rank + step, ranks)
        out_refs[step][...] = mixed_ref[:, pl.ds(pl.multiple_of(to * lanes, lanes), lanes)]


def mix(info, by_plane, by_core, arrived, gates, ranks):
    heads, width, rows = arrived.shape
    features = by_plane.shape[3]
    vmem = pl.BlockSpec(memory_space=pltpu.VMEM)
    return pl.pallas_call(
        functools.partial(mix_kernel, heads, ranks),
        in_specs=[pl.BlockSpec(memory_space=pltpu.SMEM)] + [vmem] * 4,
        out_specs=[vmem] * ranks,
        out_shape=[jax.ShapeDtypeStruct((features, rows // ranks), BF16)] * ranks,
        scratch_shapes=[pltpu.VMEM((features, features), BF16), pltpu.VMEM((features, rows), BF16)],
        compiler_params=pltpu.CompilerParams(vmem_limit_bytes=20 * MIB),
        cost_estimate=pl.CostEstimate(flops=4 * 10**9, bytes_accessed=4 * 10**6, transcendentals=0),
        name="mix",
    )(info, by_plane, by_core, gates, arrived)


def frame_at(place, rank, sizes):
    ranks = sizes[1]
    frames = FRAMES // ranks
    return lax.rem(rank - place // frames + ranks, ranks) * frames + place % frames


def pieces_kernel(info_ref, *refs):
    piece_refs, qkv_ref, out_ref = refs[:-2], refs[-2], refs[-1]
    member = info_ref[6]
    for group in range(len(piece_refs) // 2):
        for other in range(KINDS + 1):
            kind = member ^ other
            at = (other // 2, other % 2) if group % 2 == 0 else (other % 2, other // 2)
            ref = piece_refs[2 * group + at[0]]

            @pl.when(kind < KINDS)
            def projection():
                for head in range(2):
                    qkv_ref[2 * group + head, pl.ds(pl.multiple_of(kind * PAIR, 16), PAIR), :] = ref[at[1], head]

            @pl.when(kind == KINDS)
            def output():
                for head in range(2):
                    start = (2 * group + head) * PAIR
                    out_ref[start:start + PAIR, :] = ref[at[1], head]


def pieces_in_place(info, pieces):
    features = pieces[0].shape[3]
    count = features // PAIR
    vmem = pl.BlockSpec(memory_space=pltpu.VMEM)
    return pl.pallas_call(
        pieces_kernel,
        in_specs=[pl.BlockSpec(memory_space=pltpu.SMEM)] + [vmem] * len(pieces),
        out_specs=[vmem] * 2,
        out_shape=[
            jax.ShapeDtypeStruct((count, KINDS * PAIR, features), BF16),
            jax.ShapeDtypeStruct((features, features), BF16),
        ],
        compiler_params=pltpu.CompilerParams(vmem_limit_bytes=28 * MIB),
        cost_estimate=pl.CostEstimate(flops=3 * 10**9, bytes_accessed=20 * 10**6, transcendentals=0),
        name="pieces_in_place",
    )(info, *pieces)


def turned(array, span):
    lanes = array.shape[1]
    if 2 * span % 128 or span % 128 == 0:
        return [array if d == 0 else pltpu.roll(array, d * span, 1) for d in range(FRAMES)]
    odd = pltpu.roll(array, span, 1)
    found = []
    for d in range(FRAMES):
        base, shift = (odd, (d - 1) * span) if d % 2 else (array, d * span)
        whole = jnp.concatenate([base[:, lanes - shift:], base[:, :lanes - shift]], axis=1) if shift else base
        found.append(whole)
    return found


def temporal_kernel(sizes, info_ref, gates_ref, qkv_ref, last_ref, *refs):
    groups, ranks, heads, block, span, run = sizes
    mixed_refs, out_refs = refs[:ranks], refs[ranks:-3]
    normed_ref, attended_ref, result_ref = refs[-3:]
    step = pl.program_id(0)
    features, lanes = mixed_refs[0].shape
    rows = ranks * lanes
    scale = 1.0 / math.sqrt(HEAD_DIM)
    frame_count = info_ref[1]
    rank_here = info_ref[3]
    each_step = qkv_ref.shape[0] // pl.num_programs(0)

    @pl.when(step == 0)
    def norm():
        columns = flip(gates_ref[...])
        for rank in range(ranks):
            full = mixed_refs[rank][...].astype(F32)
            center = full - jnp.mean(full, axis=0, keepdims=True)
            variance = jnp.mean(center * center, axis=0, keepdims=True)
            normed = center * lax.rsqrt(variance + EPS)
            normed = normed * (1.0 + columns[:, 2:3]) + columns[:, 1:2]
            normed_ref[:, rank * lanes:(rank + 1) * lanes] = normed.astype(BF16)

    frame = lax.broadcasted_iota(jnp.int32, (FRAMES, rows), 1) // span
    delta = lax.broadcasted_iota(jnp.int32, (FRAMES, rows), 0)
    key_frame = frame_at(lax.rem(frame - delta + FRAMES, FRAMES), rank_here, sizes)
    live = key_frame < frame_count
    all_projected = [
        jnp.dot(qkv_ref[step * each_step + which], normed_ref[...], preferred_element_type=F32)
        for which in range(each_step)
    ]
    for which, projected in enumerate(all_projected):
        attended = []
        for head in range(2):
            query = projected[head * HEAD_DIM:(head + 1) * HEAD_DIM]
            key = projected[PAIR + head * HEAD_DIM:PAIR + (head + 1) * HEAD_DIM]
            value = projected[2 * PAIR + head * HEAD_DIM:2 * PAIR + (head + 1) * HEAD_DIM]
            scores = [jnp.sum(query * each, axis=0, keepdims=True) for each in turned(key, span)]
            scores = jnp.concatenate(scores, axis=0) * scale
            scores = jnp.where(live, scores, -jnp.inf)
            raised = jnp.exp(scores - jnp.max(scores, axis=0, keepdims=True))
            shares = raised / jnp.sum(raised, axis=0, keepdims=True)
            summed = None
            for d, each in enumerate(turned(value, span)):
                term = shares[d:d + 1] * each
                summed = term if summed is None else summed + term
            attended.append(summed)
        here = pl.ds(pl.multiple_of((step * each_step + which) * PAIR, PAIR), PAIR)
        attended_ref[here, :] = jnp.concatenate(attended, axis=0).astype(BF16)

    @pl.when(step == pl.num_programs(0) - 1)
    def finish():
        width = features // heads
        clip, me, count = info_ref[2], info_ref[4], info_ref[0]
        gate = flip(gates_ref[...])[:, 3:4]
        total = tn(last_ref[...], attended_ref[...])
        for rank in range(ranks):
            lane = slice(rank * lanes, (rank + 1) * lanes)
            full = mixed_refs[rank][...].astype(F32) + gate * total[:, lane]
            place = lax.broadcasted_iota(jnp.int32, (1, lanes), 1) + rank * lanes
            among = me * span + place % span
            token = (among // block * ranks + rank_here) * block + among % block
            valid = (frame_at(place // span, rank_here, sizes) < frame_count) & (token < count)
            result_ref[:, lane] = jnp.where(valid, full, 0.0).astype(BF16)
        parts = span // run
        share = max(heads // groups, 1)
        for part in range(parts):
            slot = lax.rem(part + parts - lax.rem(clip, parts), parts)
            turn = clip * share if parts == 1 else clip // parts
            for step_to in range(heads):
                to = lax.rem(me * (parts == 1) + step_to + turn, heads)
                rows_to = pl.ds(pl.multiple_of(to * width, width), width)

                def pick():
                    if parts == 1:
                        return result_ref[rows_to, :]
                    found = result_ref[rows_to, :]
                    return jnp.concatenate(
                        [found[:, f * span + part * run:f * span + (part + 1) * run] for f in range(FRAMES)], axis=1
                    )

                for each in range(parts):
                    @pl.when(slot == each)
                    def store():
                        out_refs[each * heads + step_to][...] = pick()


def temporal(info, mixed, gates, weights, sizes):
    groups, ranks, heads, block, span, run = sizes
    features, lanes = mixed[0].shape
    rows = ranks * lanes
    count = heads * (span // run)
    shape = (features // heads, FRAMES * run)
    vmem = pl.BlockSpec(memory_space=pltpu.VMEM)
    return pl.pallas_call(
        functools.partial(temporal_kernel, sizes),
        grid_spec=pltpu.PrefetchScalarGridSpec(
            num_scalar_prefetch=1,
            grid=(heads // 2,),
            in_specs=[vmem] * (3 + ranks),
            out_specs=[vmem] * count,
            scratch_shapes=[pltpu.VMEM((features, rows), BF16)] * 3,
        ),
        out_shape=[jax.ShapeDtypeStruct(shape, BF16)] * count,
        compiler_params=pltpu.CompilerParams(vmem_limit_bytes=20 * MIB),
        cost_estimate=pl.CostEstimate(flops=18 * 10**9, bytes_accessed=12 * 10**6, transcendentals=0),
        name="temporal",
    )(info, gates, *weights, *mixed)


def place_kernel(sizes, info_ref, *refs):
    groups, ranks, heads, block, span, run = sizes
    parts = span // run
    share = block // run
    piece_refs, out_ref, held_ref = refs[:-2], refs[-2], refs[-1]
    clip, rank, me = info_ref[2], info_ref[3], info_ref[4]
    for part in range(parts):
        for step in range(heads):
            if parts == 1:
                source = lax.rem(me - step + heads + groups * heads - clip * share, heads)
            else:
                source = lax.rem(me - step + heads, heads) * parts + lax.rem(clip - part + parts, parts)
            held_ref[source] = piece_refs[part * heads + step][...]
    for group in range(groups):
        for at in range(FRAMES):
            pieces = [held_ref[group * share + e, :, at * run:(at + 1) * run] for e in range(share)]
            out_ref[group * FRAMES + frame_at(at, rank, sizes)] = jnp.concatenate(pieces, axis=1) if share > 1 else pieces[0]


def place(info, pieces, sizes):
    groups, ranks, heads, block, span, run = sizes
    width, lanes = pieces[0].shape
    vmem = pl.BlockSpec(memory_space=pltpu.VMEM)
    return pl.pallas_call(
        functools.partial(place_kernel, sizes),
        in_specs=[pl.BlockSpec(memory_space=pltpu.SMEM)] + [vmem] * len(pieces),
        out_specs=vmem,
        out_shape=jax.ShapeDtypeStruct((groups * FRAMES, width, block), BF16),
        scratch_shapes=[pltpu.VMEM((len(pieces), width, lanes), BF16)],
        compiler_params=pltpu.CompilerParams(vmem_limit_bytes=12 * MIB),
        name="place",
    )(info, *pieces)


def routes(step, part, sizes):
    groups, ranks, heads, block, span, run = sizes
    parts = span // run
    share = block // run
    pairs = []
    for clip in range(groups):
        for head in range(heads):
            if parts == 1:
                to = (head // share, (head + step + clip * share) % heads)
            else:
                to = (head * parts + (part + clip) % parts, (step + clip // parts) % heads)
            pairs.append((clip * heads + head, to[0] * heads + to[1]))
    return pairs


def on_device(
    shape, spatial_qkv, stream, out_spatial, qkv_temporal, out_temporal, modulation, tok_count, frame_count
):
    outer, clips_inner, rank_hi, cores, heads = shape
    groups = outer * clips_inner
    ranks = rank_hi * cores
    assert cores == 2 and clips_inner * rank_hi == KINDS + 1
    clip = lax.axis_index(("outer", "clip"))
    rank = lax.axis_index(("rank", "core"))
    core = lax.axis_index("core")
    head = lax.axis_index("head")
    member = lax.axis_index(("clip", "rank"))
    width = spatial_qkv.shape[3]
    features = out_spatial.shape[1]
    frames, tokens = stream.shape[:2]
    block = tokens // (groups * ranks)
    span = tokens // (ranks * heads)
    run = min(block, span)
    sizes = (groups, ranks, heads, block, span, run)

    def send(array, axis, size, step):
        return lax.ppermute(array, axis, [(i, (i + step) % size) for i in range(size)])

    def around(arrays, axis, size):
        return [arrays[0]] + [send(arrays[k], axis, size, k) for k in range(1, size)]

    def swap(array, axis, size, bit):
        return lax.ppermute(array, axis, [(i, i ^ bit) for i in range(size)])

    info = jnp.stack([tok_count[clip], frame_count[clip], clip, rank, head, core, member]).astype(jnp.int32)
    here = lax.dynamic_index_in_dim(modulation, clip, 0, keepdims=False)
    gates = jnp.concatenate([here, here], axis=0)

    plane = clips_inner * rank_hi
    turned = jnp.swapaxes(qkv_temporal, 1, 2)
    weight = lax.dynamic_slice(turned, (jnp.minimum(member, KINDS - 1), core * PAIR, 0), (1, PAIR, features))[0]
    other = lax.dynamic_slice(out_temporal, (core * PAIR, 0), (PAIR, features))
    weight = jnp.where(member < KINDS, weight, other)
    half = width // cores
    strip = half // KINDS
    spatial = lax.dynamic_slice(
        out_spatial, (core * half + jnp.minimum(member, KINDS - 1) * strip, 0), (strip, features)
    )
    spatial, info, weight = lax.optimization_barrier((spatial, info, weight))

    mine = around([weight] * heads, "head", heads)
    *arranged, rows = arrange(jnp.swapaxes(spatial_qkv, 2, 3), jnp.swapaxes(stream, 1, 2), sizes)
    early = spatial_attention(info, *arranged, ranks, 0, heads - 1)
    mine, early, spatial = lax.optimization_barrier((mine, early, spatial))

    first = [jnp.stack(pair) for pair in (mine[:2], mine[2:])]
    second = [swap(part, ("clip", "rank"), plane, bit) for part, bit in zip(first, (1, 2))]
    strips = around([spatial] * heads, "head", heads)
    first, info = lax.optimization_barrier((first, info))
    attended = spatial_attention(info, *arranged, ranks, heads - 1, 1, early, rows)
    first, second, strips, attended = lax.optimization_barrier((first, second, strips, attended))

    arrived = lax.all_to_all(attended, "head", 0, 0)
    pieces = []
    for near, far, bit in zip(first, second, (2, 1)):
        part = jnp.stack([near, far])
        pieces += [part, swap(part, ("clip", "rank"), plane, bit)]
    same = jnp.stack(strips)
    by_plane = jnp.stack([same] + [swap(same, ("clip", "rank"), plane, bit) for bit in range(1, plane)])
    by_core = swap(by_plane, "core", cores, 1)
    pieces += [swap(each, "core", cores, 1) for each in pieces]
    mixed = mix(info, by_plane, by_core, arrived, gates, ranks)
    mixed = around(mixed, ("rank", "core"), ranks)
    result = temporal(info, mixed, gates, pieces_in_place(info, pieces), sizes)
    arrived = [
        lax.ppermute(result[part * heads + step], ("outer", "clip", "head"), routes(step, part, sizes))
        for part in range(span // run) for step in range(heads)
    ]
    return jnp.swapaxes(place(info, arrived, sizes), 1, 2)


def solution(mesh):
    seq, heads = mesh.shape["seq"], mesh.shape["head"]

    def whole(spatial_qkv, stream, *rest):
        frames = spatial_qkv.shape[1] // seq
        ranks = FRAMES // frames
        clips_inner = SLICES // ranks
        shape = (seq // SLICES, clips_inner, ranks // 2, 2, heads)
        fine = Mesh(mesh.devices.reshape(shape), ("outer", "clip", "rank", "core", "head"))
        split = ("outer", "clip", "rank", "core")
        in_specs = (
            P(None, split, None, "head"),
            P(split, None, "head"),
            P("head", None),
            P(None, None, "head"),
            P("head", None),
            P(),
            P(),
            P(),
        )
        return jax.shard_map(
            functools.partial(on_device, shape), mesh=fine, in_specs=in_specs, out_specs=P(None, split, "head"),
            check_vma=False,
        )(spatial_qkv, stream, *rest)

    return whole
```

```python
import functools
import math

import jax
import jax.numpy as jnp
from jax import lax
from jax.experimental import pallas as pl
from jax.experimental.pallas import tpu as pltpu
from jax.sharding import Mesh
from jax.sharding import PartitionSpec as P

HEAD_DIM = 72
FRAMES = 8
PAIR = 2 * HEAD_DIM
KINDS = 3
SLICES = 8
EPS = 1e-6
F32 = jnp.float32
BF16 = jnp.bfloat16
MIB = 1024 * 1024


def flip(array):
    return jnp.swapaxes(array, 0, 1)


def tn(lhs, rhs):
    return lax.dot_general(lhs, rhs, (((0,), (0,)), ((), ())), preferred_element_type=F32)


def runs_of(chunk, rank, sizes):
    groups, ranks, heads, block, span, run = sizes
    starts = []
    for piece in range(span // run):
        place = chunk * span + piece * run
        starts.append((place // block * ranks + rank) * block + place % block)
    return starts


def arrange_kernel(sizes, qkv_ref, stream_ref, query_ref, key_ref, value_ref, rows_ref):
    groups, ranks, heads, block, span, run = sizes
    _, frames, width, tokens = qkv_ref.shape
    for each in range(heads):
        for frame in range(frames):
            pieces = [
                qkv_ref[0, frame, :, start:start + run]
                for rank in range(ranks) for start in runs_of(each, rank, sizes)
            ]
            gathered = jnp.concatenate(pieces, axis=1)
            for pair in range(width // PAIR):
                query_ref[each, frame, pair] = gathered[pair * PAIR:(pair + 1) * PAIR]
        pieces = [
            stream_ref[frame, :, start:start + run]
            for rank in range(ranks) for frame in range(frames) for start in runs_of(each, rank, sizes)
        ]
        rows_ref[each] = jnp.concatenate(pieces, axis=1)
    for frame in range(frames):
        for pair in range(width // PAIR):
            keys = qkv_ref[1, frame, pair * PAIR:(pair + 1) * PAIR, :]
            key_ref[frame, pair] = flip(keys.astype(F32)).astype(BF16)
            value_ref[frame, pair, :PAIR, :] = qkv_ref[2, frame, pair * PAIR:(pair + 1) * PAIR, :]
            value_ref[frame, pair, PAIR:, :] = jnp.ones((value_ref.shape[2] - PAIR, tokens), BF16)


def arrange(qkv, stream, sizes):
    heads = sizes[2]
    _, frames, width, tokens = qkv.shape
    shapes = [
        (heads, frames, width // PAIR, PAIR, tokens // heads),
        (frames, width // PAIR, tokens, PAIR),
        (frames, width // PAIR, PAIR + 16, tokens),
        (heads, width, frames * tokens // heads),
    ]
    vmem = pl.BlockSpec(memory_space=pltpu.VMEM)
    return pl.pallas_call(
        functools.partial(arrange_kernel, sizes),
        in_specs=[vmem] * 2,
        out_specs=[vmem] * len(shapes),
        out_shape=[jax.ShapeDtypeStruct(shape, BF16) for shape in shapes],
        compiler_params=pltpu.CompilerParams(vmem_limit_bytes=16 * MIB),
        cost_estimate=pl.CostEstimate(flops=6 * 10**9, bytes_accessed=5 * 10**6, transcendentals=0),
        name="arrange",
    )(qkv, stream)


def spatial_kernel(ranks, first, info_ref, query_ref, key_ref, value_ref, *refs):
    held_refs, out_ref, part_ref = refs[:-2], refs[-2], refs[-1]
    turn = pl.program_id(0)
    chunk = turn + first
    to = chunk if held_refs else turn
    _, frames, pairs, _, per_frame = query_ref.shape
    tokens = key_ref.shape[2]
    width = pairs * PAIR
    span = per_frame // ranks
    scale = math.log2(math.e) / math.sqrt(HEAD_DIM)
    count = info_ref[0]

    def attend(keys, masked):
        def of_pair(at, carry):
            frame, pair = at // pairs, at % pairs
            row = lax.broadcasted_iota(jnp.int32, (PAIR, per_frame), 0)
            queries = query_ref[chunk, frame, pair]
            for head in range(2):
                mine = (row >= head * HEAD_DIM) & (row < (head + 1) * HEAD_DIM)
                query = jnp.where(mine, queries, jnp.zeros((), BF16))
                scores = jnp.dot(key_ref[frame, pair, :keys, :], query, preferred_element_type=F32)
                if masked:
                    token = lax.broadcasted_iota(jnp.int32, (keys, per_frame), 0)
                    scores = jnp.where(token < count, scores, -jnp.inf)
                highest = jnp.max(scores, axis=0, keepdims=True)
                raised = jnp.exp2(scores * scale - highest * scale).astype(BF16)
                summed = jnp.dot(value_ref[frame, pair, :, :keys], raised, preferred_element_type=F32)
                inside = slice(head * HEAD_DIM, (head + 1) * HEAD_DIM)
                part_ref[frame, pair, inside, :] = summed[inside] / summed[PAIR:PAIR + 1]
            return carry

        lax.fori_loop(0, frames * pairs, of_pair, 0)

    half = tokens // 2

    @pl.when(count >= tokens)
    def whole():
        attend(tokens, False)

    @pl.when((count < tokens) & (count > half))
    def some():
        attend(tokens, True)

    @pl.when(count <= half)
    def few():
        attend(half, True)

    for pair in range(pairs):
        pieces = [
            part_ref[frame, pair, :, rank * span:(rank + 1) * span] for rank in range(ranks) for frame in range(frames)
        ]
        out_ref[to, pair * PAIR:(pair + 1) * PAIR, :] = jnp.concatenate(pieces, axis=1).astype(BF16)
    if held_refs:
        @pl.when(turn == 0)
        def join():
            out_ref[:first, :width, :] = held_refs[0][...]
            out_ref[:, width:, :] = held_refs[1][...]


def spatial_attention(info, queries, keys, values, ranks, first, count, *held):
    heads, frames, pairs, _, per_frame = queries.shape
    shape = (heads, 2 * pairs * PAIR, frames * per_frame) if held else (count, pairs * PAIR, frames * per_frame)
    vmem = pl.BlockSpec(memory_space=pltpu.VMEM)
    return pl.pallas_call(
        functools.partial(spatial_kernel, ranks, first),
        grid_spec=pltpu.PrefetchScalarGridSpec(
            num_scalar_prefetch=1,
            grid=(count,),
            in_specs=[vmem] * (3 + len(held)),
            out_specs=vmem,
            scratch_shapes=[pltpu.VMEM((frames, pairs, PAIR, per_frame), F32)],
        ),
        out_shape=jax.ShapeDtypeStruct(shape, BF16),
        compiler_params=pltpu.CompilerParams(vmem_limit_bytes=16 * MIB),
        cost_estimate=pl.CostEstimate(flops=14 * 10**9, bytes_accessed=5 * 10**6, transcendentals=4 * 10**6),
        name="spatial_attention",
    )(info, queries, keys, values, *held)


def mix_kernel(heads, ranks, info_ref, plane_ref, core_ref, gates_ref, rows_ref, *refs):
    out_refs, weight_ref, mixed_ref = refs[:-2], refs[-2], refs[-1]
    rank, me, core, member = info_ref[3], info_ref[4], info_ref[5], info_ref[6]
    members, _, strip, _ = plane_ref.shape
    width = rows_ref.shape[1] // 2
    half = width // 2
    last = half // strip - 1
    gate = flip(gates_ref[...])[:, 0:1]
    for far, ref in enumerate((plane_ref, core_ref)):
        for other in range(members):
            whose = jnp.minimum(member ^ other, last)
            for step in range(heads):
                source = lax.rem(me - step + heads, heads)
                start = source * width + (core ^ far) * half + whose * strip
                weight_ref[pl.ds(pl.multiple_of(start, 16), strip), :] = ref[other, step]
    summed = None
    for source in range(heads):
        term = tn(weight_ref[source * width:(source + 1) * width, :], rows_ref[source, :width, :])
        summed = term if summed is None else summed + term
    for source in range(heads):
        here = slice(source * width, (source + 1) * width)
        mixed = rows_ref[source, width:, :].astype(F32) + gate[here] * summed[here]
        mixed_ref[here, :] = mixed.astype(BF16)
    lanes = mixed_ref.shape[1] // ranks
    for step in range(ranks):
        to = lax.rem(rank + step, ranks)
        out_refs[step][...] = mixed_ref[:, pl.ds(pl.multiple_of(to * lanes, lanes), lanes)]


def mix(info, by_plane, by_core, arrived, gates, ranks):
    heads, width, rows = arrived.shape
    features = by_plane.shape[3]
    vmem = pl.BlockSpec(memory_space=pltpu.VMEM)
    return pl.pallas_call(
        functools.partial(mix_kernel, heads, ranks),
        in_specs=[pl.BlockSpec(memory_space=pltpu.SMEM)] + [vmem] * 4,
        out_specs=[vmem] * ranks,
        out_shape=[jax.ShapeDtypeStruct((features, rows // ranks), BF16)] * ranks,
        scratch_shapes=[pltpu.VMEM((features, features), BF16), pltpu.VMEM((features, rows), BF16)],
        compiler_params=pltpu.CompilerParams(vmem_limit_bytes=20 * MIB),
        cost_estimate=pl.CostEstimate(flops=4 * 10**9, bytes_accessed=4 * 10**6, transcendentals=0),
        name="mix",
    )(info, by_plane, by_core, gates, arrived)


def frame_at(place, rank, sizes):
    ranks = sizes[1]
    frames = FRAMES // ranks
    return lax.rem(rank - place // frames + ranks, ranks) * frames + place % frames


def pieces_kernel(info_ref, *refs):
    piece_refs, qkv_ref, out_ref = refs[:-2], refs[-2], refs[-1]
    member = info_ref[6]
    for group in range(len(piece_refs) // 2):
        for other in range(KINDS + 1):
            kind = member ^ other
            at = (other // 2, other % 2) if group % 2 == 0 else (other % 2, other // 2)
            ref = piece_refs[2 * group + at[0]]

            @pl.when(kind < KINDS)
            def projection():
                for head in range(2):
                    qkv_ref[2 * group + head, pl.ds(pl.multiple_of(kind * PAIR, 16), PAIR), :] = ref[at[1], head]

            @pl.when(kind == KINDS)
            def output():
                for head in range(2):
                    start = (2 * group + head) * PAIR
                    out_ref[start:start + PAIR, :] = ref[at[1], head]


def pieces_in_place(info, pieces):
    features = pieces[0].shape[3]
    count = features // PAIR
    vmem = pl.BlockSpec(memory_space=pltpu.VMEM)
    return pl.pallas_call(
        pieces_kernel,
        in_specs=[pl.BlockSpec(memory_space=pltpu.SMEM)] + [vmem] * len(pieces),
        out_specs=[vmem] * 2,
        out_shape=[
            jax.ShapeDtypeStruct((count, KINDS * PAIR, features), BF16),
            jax.ShapeDtypeStruct((features, features), BF16),
        ],
        compiler_params=pltpu.CompilerParams(vmem_limit_bytes=28 * MIB),
        cost_estimate=pl.CostEstimate(flops=3 * 10**9, bytes_accessed=20 * 10**6, transcendentals=0),
        name="pieces_in_place",
    )(info, *pieces)


def turned(array, span):
    lanes = array.shape[1]
    if 2 * span % 128 or span % 128 == 0:
        return [array if d == 0 else pltpu.roll(array, d * span, 1) for d in range(FRAMES)]
    odd = pltpu.roll(array, span, 1)
    found = []
    for d in range(FRAMES):
        base, shift = (odd, (d - 1) * span) if d % 2 else (array, d * span)
        whole = jnp.concatenate([base[:, lanes - shift:], base[:, :lanes - shift]], axis=1) if shift else base
        found.append(whole)
    return found


def temporal_kernel(sizes, info_ref, gates_ref, qkv_ref, last_ref, *refs):
    groups, ranks, heads, block, span, run = sizes
    mixed_refs, out_refs = refs[:ranks], refs[ranks:-3]
    normed_ref, attended_ref, result_ref = refs[-3:]
    step = pl.program_id(0)
    features, lanes = mixed_refs[0].shape
    rows = ranks * lanes
    scale = 1.0 / math.sqrt(HEAD_DIM)
    frame_count = info_ref[1]
    rank_here = info_ref[3]
    each_step = qkv_ref.shape[0] // pl.num_programs(0)

    @pl.when(step == 0)
    def norm():
        columns = flip(gates_ref[...])
        for rank in range(ranks):
            full = mixed_refs[rank][...].astype(F32)
            center = full - jnp.mean(full, axis=0, keepdims=True)
            variance = jnp.mean(center * center, axis=0, keepdims=True)
            normed = center * lax.rsqrt(variance + EPS)
            normed = normed * (1.0 + columns[:, 2:3]) + columns[:, 1:2]
            normed_ref[:, rank * lanes:(rank + 1) * lanes] = normed.astype(BF16)

    frame = lax.broadcasted_iota(jnp.int32, (FRAMES, rows), 1) // span
    delta = lax.broadcasted_iota(jnp.int32, (FRAMES, rows), 0)
    key_frame = frame_at(lax.rem(frame - delta + FRAMES, FRAMES), rank_here, sizes)
    live = key_frame < frame_count
    all_projected = [
        jnp.dot(qkv_ref[step * each_step + which], normed_ref[...], preferred_element_type=F32)
        for which in range(each_step)
    ]
    for which, projected in enumerate(all_projected):
        attended = []
        for head in range(2):
            query = projected[head * HEAD_DIM:(head + 1) * HEAD_DIM]
            key = projected[PAIR + head * HEAD_DIM:PAIR + (head + 1) * HEAD_DIM]
            value = projected[2 * PAIR + head * HEAD_DIM:2 * PAIR + (head + 1) * HEAD_DIM]
            scores = [jnp.sum(query * each, axis=0, keepdims=True) for each in turned(key, span)]
            scores = jnp.concatenate(scores, axis=0) * scale
            scores = jnp.where(live, scores, -jnp.inf)
            raised = jnp.exp(scores - jnp.max(scores, axis=0, keepdims=True))
            shares = raised / jnp.sum(raised, axis=0, keepdims=True)
            summed = None
            for d, each in enumerate(turned(value, span)):
                term = shares[d:d + 1] * each
                summed = term if summed is None else summed + term
            attended.append(summed)
        here = pl.ds(pl.multiple_of((step * each_step + which) * PAIR, PAIR), PAIR)
        attended_ref[here, :] = jnp.concatenate(attended, axis=0).astype(BF16)

    @pl.when(step == pl.num_programs(0) - 1)
    def finish():
        width = features // heads
        clip, me, count = info_ref[2], info_ref[4], info_ref[0]
        gate = flip(gates_ref[...])[:, 3:4]
        total = tn(last_ref[...], attended_ref[...])
        for rank in range(ranks):
            lane = slice(rank * lanes, (rank + 1) * lanes)
            full = mixed_refs[rank][...].astype(F32) + gate * total[:, lane]
            place = lax.broadcasted_iota(jnp.int32, (1, lanes), 1) + rank * lanes
            among = me * span + place % span
            token = (among // block * ranks + rank_here) * block + among % block
            valid = (frame_at(place // span, rank_here, sizes) < frame_count) & (token < count)
            result_ref[:, lane] = jnp.where(valid, full, 0.0).astype(BF16)
        parts = span // run
        share = max(heads // groups, 1)
        for part in range(parts):
            slot = lax.rem(part + parts - lax.rem(clip, parts), parts)
            turn = clip * share if parts == 1 else clip // parts
            for step_to in range(heads):
                to = lax.rem(me * (parts == 1) + step_to + turn, heads)
                rows_to = pl.ds(pl.multiple_of(to * width, width), width)

                def pick():
                    if parts == 1:
                        return result_ref[rows_to, :]
                    found = result_ref[rows_to, :]
                    return jnp.concatenate(
                        [found[:, f * span + part * run:f * span + (part + 1) * run] for f in range(FRAMES)], axis=1
                    )

                for each in range(parts):
                    @pl.when(slot == each)
                    def store():
                        out_refs[each * heads + step_to][...] = pick()


def temporal(info, mixed, gates, weights, sizes):
    groups, ranks, heads, block, span, run = sizes
    features, lanes = mixed[0].shape
    rows = ranks * lanes
    count = heads * (span // run)
    shape = (features // heads, FRAMES * run)
    vmem = pl.BlockSpec(memory_space=pltpu.VMEM)
    return pl.pallas_call(
        functools.partial(temporal_kernel, sizes),
        grid_spec=pltpu.PrefetchScalarGridSpec(
            num_scalar_prefetch=1,
            grid=(heads // 2,),
            in_specs=[vmem] * (3 + ranks),
            out_specs=[vmem] * count,
            scratch_shapes=[pltpu.VMEM((features, rows), BF16)] * 3,
        ),
        out_shape=[jax.ShapeDtypeStruct(shape, BF16)] * count,
        compiler_params=pltpu.CompilerParams(vmem_limit_bytes=20 * MIB),
        cost_estimate=pl.CostEstimate(flops=18 * 10**9, bytes_accessed=12 * 10**6, transcendentals=0),
        name="temporal",
    )(info, gates, *weights, *mixed)


def place_kernel(sizes, info_ref, *refs):
    groups, ranks, heads, block, span, run = sizes
    parts = span // run
    share = block // run
    piece_refs, out_ref, held_ref = refs[:-2], refs[-2], refs[-1]
    clip, rank, me = info_ref[2], info_ref[3], info_ref[4]
    group = pl.program_id(0)

    @pl.when(group == 0)
    def hold():
        for part in range(parts):
            for step in range(heads):
                if parts == 1:
                    source = lax.rem(me - step + heads + groups * heads - clip * share, heads)
                else:
                    source = lax.rem(me - step + heads, heads) * parts + lax.rem(clip - part + parts, parts)
                held_ref[source] = piece_refs[part * heads + step][...]

    for at in range(FRAMES):
        pieces = [held_ref[group * share + e, :, at * run:(at + 1) * run] for e in range(share)]
        out_ref[frame_at(at, rank, sizes)] = jnp.concatenate(pieces, axis=1) if share > 1 else pieces[0]


def place(info, pieces, sizes):
    groups, ranks, heads, block, span, run = sizes
    width, lanes = pieces[0].shape
    vmem = pl.BlockSpec(memory_space=pltpu.VMEM)
    return pl.pallas_call(
        functools.partial(place_kernel, sizes),
        in_specs=[pl.BlockSpec(memory_space=pltpu.SMEM)] + [vmem] * len(pieces),
        out_specs=pl.BlockSpec((FRAMES, width, block), lambda g: (g, 0, 0)),
        grid=(groups,),
        out_shape=jax.ShapeDtypeStruct((groups * FRAMES, width, block), BF16),
        scratch_shapes=[pltpu.VMEM((len(pieces), width, lanes), BF16)],
        compiler_params=pltpu.CompilerParams(vmem_limit_bytes=12 * MIB),
        name="place",
    )(info, *pieces)


def routes(step, part, sizes):
    groups, ranks, heads, block, span, run = sizes
    parts = span // run
    share = block // run
    pairs = []
    for clip in range(groups):
        for head in range(heads):
            if parts == 1:
                to = (head // share, (head + step + clip * share) % heads)
            else:
                to = (head * parts + (part + clip) % parts, (step + clip // parts) % heads)
            pairs.append((clip * heads + head, to[0] * heads + to[1]))
    return pairs


def on_device(
    shape, spatial_qkv, stream, out_spatial, qkv_temporal, out_temporal, modulation, tok_count, frame_count
):
    outer, clips_inner, rank_hi, cores, heads = shape
    groups = outer * clips_inner
    ranks = rank_hi * cores
    assert cores == 2 and clips_inner * rank_hi == KINDS + 1
    clip = lax.axis_index(("outer", "clip"))
    rank = lax.axis_index(("rank", "core"))
    core = lax.axis_index("core")
    head = lax.axis_index("head")
    member = lax.axis_index(("clip", "rank"))
    width = spatial_qkv.shape[3]
    features = out_spatial.shape[1]
    frames, tokens = stream.shape[:2]
    block = tokens // (groups * ranks)
    span = tokens // (ranks * heads)
    run = min(block, span)
    sizes = (groups, ranks, heads, block, span, run)

    def send(array, axis, size, step):
        return lax.ppermute(array, axis, [(i, (i + step) % size) for i in range(size)])

    def around(arrays, axis, size):
        return [arrays[0]] + [send(arrays[k], axis, size, k) for k in range(1, size)]

    def swap(array, axis, size, bit):
        return lax.ppermute(array, axis, [(i, i ^ bit) for i in range(size)])

    info = jnp.stack([tok_count[clip], frame_count[clip], clip, rank, head, core, member]).astype(jnp.int32)
    here = lax.dynamic_index_in_dim(modulation, clip, 0, keepdims=False)
    gates = jnp.concatenate([here, here], axis=0)

    plane = clips_inner * rank_hi
    turned = jnp.swapaxes(qkv_temporal, 1, 2)
    weight = lax.dynamic_slice(turned, (jnp.minimum(member, KINDS - 1), core * PAIR, 0), (1, PAIR, features))[0]
    other = lax.dynamic_slice(out_temporal, (core * PAIR, 0), (PAIR, features))
    weight = jnp.where(member < KINDS, weight, other)
    half = width // cores
    strip = half // KINDS
    spatial = lax.dynamic_slice(
        out_spatial, (core * half + jnp.minimum(member, KINDS - 1) * strip, 0), (strip, features)
    )
    spatial, info, weight = lax.optimization_barrier((spatial, info, weight))

    mine = around([weight] * heads, "head", heads)
    *arranged, rows = arrange(jnp.swapaxes(spatial_qkv, 2, 3), jnp.swapaxes(stream, 1, 2), sizes)
    early = spatial_attention(info, *arranged, ranks, 0, heads - 1)
    mine, early, spatial = lax.optimization_barrier((mine, early, spatial))

    first = [jnp.stack(pair) for pair in (mine[:2], mine[2:])]
    second = [swap(part, ("clip", "rank"), plane, bit) for part, bit in zip(first, (1, 2))]
    strips = around([spatial] * heads, "head", heads)
    first, info = lax.optimization_barrier((first, info))
    attended = spatial_attention(info, *arranged, ranks, heads - 1, 1, early, rows)
    first, second, strips, attended = lax.optimization_barrier((first, second, strips, attended))

    arrived = lax.all_to_all(attended, "head", 0, 0)
    pieces = []
    for near, far, bit in zip(first, second, (2, 1)):
        part = jnp.stack([near, far])
        pieces += [part, swap(part, ("clip", "rank"), plane, bit)]
    same = jnp.stack(strips)
    by_plane = jnp.stack([same] + [swap(same, ("clip", "rank"), plane, bit) for bit in range(1, plane)])
    by_core = swap(by_plane, "core", cores, 1)
    pieces += [swap(each, "core", cores, 1) for each in pieces]
    mixed = mix(info, by_plane, by_core, arrived, gates, ranks)
    mixed = around(mixed, ("rank", "core"), ranks)
    result = temporal(info, mixed, gates, pieces_in_place(info, pieces), sizes)
    arrived = [
        lax.ppermute(result[part * heads + step], ("outer", "clip", "head"), routes(step, part, sizes))
        for part in range(span // run) for step in range(heads)
    ]
    return jnp.swapaxes(place(info, arrived, sizes), 1, 2)


def solution(mesh):
    seq, heads = mesh.shape["seq"], mesh.shape["head"]

    def whole(spatial_qkv, stream, *rest):
        frames = spatial_qkv.shape[1] // seq
        ranks = FRAMES // frames
        clips_inner = SLICES // ranks
        shape = (seq // SLICES, clips_inner, ranks // 2, 2, heads)
        fine = Mesh(mesh.devices.reshape(shape), ("outer", "clip", "rank", "core", "head"))
        split = ("outer", "clip", "rank", "core")
        in_specs = (
            P(None, split, None, "head"),
            P(split, None, "head"),
            P("head", None),
            P(None, None, "head"),
            P("head", None),
            P(),
            P(),
            P(),
        )
        return jax.shard_map(
            functools.partial(on_device, shape), mesh=fine, in_specs=in_specs, out_specs=P(None, split, "head"),
            check_vma=False,
        )(spatial_qkv, stream, *rest)

    return whole
```
